128 devices in a mesh: row: 16 (over y, z_lo, core), col: 8 (over z_hi, x).
Axes of the slice: x: 4, y: 4, z: 4 (z_hi: 2, z_lo: 2; z = z_hi * 2 + z_lo), core: 2. Of those that a mesh axis runs over, the one named last changes fastest.
Arguments:
- images: bfloat16 [24576, 768], P(('row', 'col')), may hold values from -2 to 2
- texts: bfloat16 [24576, 768], P(('col', 'row')), may hold values from -3.5 to 3.5
- pair_index: int32 [24576], P(('row', 'col')), may hold values from 0 to 24575, as said below
- log_scale: float32 [1], replicated, may hold values from 3.87 to 4.16
- bias: float32 [1], replicated, may hold values from -12 to -10
Outputs:
- loss: float32 [1], replicated
- grad_images: float32 [24576, 768], P(('row', 'col'))
- grad_texts: float32 [24576, 768], P(('col', 'row'))
The draws below stay inside these ranges and needn't reach their ends.
Inputs may be any that keep to these rules, and one draw needn't show every extreme that they name: `pair_index`: every text row is paired with exactly one image row.
All inputs are finite; a program needn't handle non-finite values.
Results may differ from the reference program's by a relative error of at most 0.0051.
Values may be sent and summed in bfloat16 or wider, within the bound.
No kernel may reach another device: no remote copies, remote signals or barrier semaphores. Data moves between devices by JAX's collectives and lax.ppermute only.
A program may use at most 128 MiB of HBM per device.

```python
import math
import jax
import jax.numpy as jnp
from jax import lax

D = 768
ROWS_DEV = 192
BATCH = 24576
N_ROW = 16
N_COL = 8


def shared_rows(key):
    order = jax.random.permutation(jax.random.fold_in(key, 101), BATCH).astype(jnp.int32)
    noise = jnp.clip(jax.random.normal(jax.random.fold_in(key, 102), (BATCH, D), jnp.float32), -5.0, 5.0)
    base = noise
    position = jnp.arange(BATCH, dtype=jnp.float32) / BATCH
    jitter = jax.random.uniform(jax.random.fold_in(key, 104), (BATCH,), jnp.float32, 1.0, 1.5)
    strength = 0.1 * jnp.exp2(2.6 * position) * jitter
    return (order, base, strength)


def draw_pair_index(key, part):
    order, base, strength = shared_rows(key)
    return order


def draw_images(key, part):
    order, base, strength = shared_rows(key)
    values = base * (1.4 / math.sqrt(D))
    return jnp.clip(values, -2.0, 2.0).astype(jnp.bfloat16)


def draw_texts(key, part):
    order, base, strength = shared_rows(key)
    key = jax.random.fold_in(key, 2)
    noise = jnp.clip(jax.random.normal(jax.random.fold_in(key, 1), (BATCH, D), jnp.float32), -5.0, 5.0)
    placed = jnp.zeros((BATCH, D), jnp.float32).at[order].set(strength[:, None] * base)
    values = (placed + noise) * (1.4 / math.sqrt(D))
    return jnp.clip(values, -3.5, 3.5).astype(jnp.bfloat16)


def setup_inputs(seed: int = 0) -> dict:
    splits = jax.random.split(jax.random.key(seed), 6)
    images = draw_images(jax.random.fold_in(splits[5], 71), 0)
    texts = draw_texts(jax.random.fold_in(splits[5], 71), 0)
    pair_index = draw_pair_index(jax.random.fold_in(splits[5], 71), 0)
    log_scale = jnp.clip(jax.random.uniform(splits[3], (1,), jnp.float32, 3.87, 4.16), 3.87, 4.16)
    bias = jnp.clip(jax.random.uniform(splits[4], (1,), jnp.float32, -12.0, -10.0), -12.0, -10.0)
    return {"images": images, "texts": texts, "pair_index": pair_index, "log_scale": log_scale, "bias": bias}


EPS = 1e-06

def normalize(values):
    wide = values.astype(jnp.float32)
    inverse = lax.rsqrt(lax.optimization_barrier(jnp.sum(wide * wide, axis=-1, keepdims=True)) + EPS)
    return (wide * inverse, inverse)

def unproject(grad_unit, unit, inverse):
    along = lax.optimization_barrier(jnp.sum(grad_unit * unit, axis=-1, keepdims=True))
    return (grad_unit - unit * along) * inverse

def reference(images, texts, pair_index, log_scale, bias):
    x_unit, inv_x = normalize(images)
    y_unit, inv_y = normalize(texts)
    x_low = x_unit.astype(jnp.bfloat16)
    y_low = y_unit.astype(jnp.bfloat16)
    scale = jnp.exp(log_scale[0])
    shift = bias[0]
    columns = jnp.arange(BATCH, dtype=jnp.int32)
    block = ROWS_DEV * N_COL

    def step(carry, item):
        grad_y, total = carry
        x_block, pair_block = item
        score = jnp.dot(x_block, y_low.T, preferred_element_type=jnp.float32)
        logit = scale * score + shift
        sign = jnp.where(pair_block[:, None] == columns[None, :], 1.0, -1.0).astype(jnp.float32)
        total = total - jnp.sum(jax.nn.log_sigmoid(sign * logit))
        weight = (-scale * sign * jax.nn.sigmoid(-sign * logit)).astype(jnp.bfloat16)
        grad_x = jnp.dot(weight, y_low, preferred_element_type=jnp.float32)
        grad_y = grad_y + jnp.dot(weight.T, x_block, preferred_element_type=jnp.float32)
        return ((grad_y, total), grad_x)
    start = (jnp.zeros((BATCH, D), jnp.float32), jnp.zeros((), jnp.float32))
    (gy_unit, total), gx_blocks = lax.scan(step, start, (x_low.reshape(N_ROW, block, D), pair_index.reshape(N_ROW, block)))
    gx_unit = gx_blocks.reshape(BATCH, D)
    loss = (total / BATCH).reshape(1)
    return (loss, unproject(gx_unit, x_unit, inv_x), unproject(gy_unit, y_unit, inv_y))
```

```python
import functools

import jax
import jax.numpy as jnp
from jax import lax
from jax.experimental import pallas as pl
from jax.experimental.pallas import tpu as pltpu
from jax.sharding import PartitionSpec as P

EPS = 1e-06
LOG2E = 1.4426950408889634
N_ROW = 16
N_COL = 8
R = 192
D = 768
RX = R + 16
NX = R * N_COL
NY = R * N_ROW
BM = 512
NT = (((1,), (1,)), ((), ()))
TN = (((0,), (0,)), ((), ()))
VMEM = pl.BlockSpec(memory_space=pltpu.VMEM)
SMEM = pl.BlockSpec(memory_space=pltpu.SMEM)


def row_pairs(dy, dz, dc):
    out = []
    for r in range(N_ROW):
        y, z, c = r // 4, (r // 2) % 2, r % 2
        out.append((r, (((y + dy) % 4) * 2 + (z ^ dz)) * 2 + (c ^ dc)))
    return out


def col_pairs(dx, dz):
    return [(c, ((c // 4) ^ dz) * 4 + (c % 4 + dx) % 4) for c in range(N_COL)]


def send_row(value, dy=0, dz=0, dc=0):
    return lax.ppermute(value, "row", row_pairs(dy, dz, dc))


def send_col(value, dx=0, dz=0):
    return lax.ppermute(value, "col", col_pairs(dx, dz))


def normalize(ref):
    wide = ref[...].astype(jnp.float32)
    inverse = lax.rsqrt(jnp.sum(wide * wide, axis=-1, keepdims=True) + EPS)
    return wide * inverse, inverse


def prep_kernel(images_ref, texts_ref, pair_ref, x_ref, y_ref):
    x_ref[:R, :] = normalize(images_ref)[0].astype(jnp.bfloat16)
    y_ref[...] = normalize(texts_ref)[0].astype(jnp.bfloat16)
    x_ref[R:, :] = jnp.broadcast_to(pair_ref[...], (16, D)).astype(jnp.bfloat16)


def score_kernel(*refs):
    sc_ref, at_ref = refs[:2]
    xs = refs[2 : 2 + N_COL]
    ys = refs[2 + N_COL : 2 + N_COL + N_ROW]
    gx_out, gy_own, gy_sib, loss_ref, x_all, y_all, place, gx_acc, loss_acc = refs[2 + N_COL + N_ROW :]
    col, row_y, row_z, row_c = at_ref[0], at_ref[1], at_ref[2], at_ref[3]
    slope, shift, scale = sc_ref[0], sc_ref[1], sc_ref[2]
    for k, ref in enumerate(xs):
        x_all[k * R : (k + 1) * R, :] = ref[:R, :]
        tail = ref[R : R + 16, :].astype(jnp.float32).astype(jnp.int32)[:1, :]
        shard, offset = tail[:, :R], tail[:, 256 : 256 + R]
        rel = (
            ((shard & 1) ^ row_c) * 8
            + (((shard >> 2) - row_y) & 3) * 2
            + (((shard >> 1) & 1) ^ row_z)
        )
        place[:, k * R : (k + 1) * R] = jnp.where((shard >> 4) == col, rel * R + offset, -1)
    for k, ref in enumerate(ys):
        y_all[k * R : (k + 1) * R, :] = ref[...]
    gx_acc[...] = jnp.zeros_like(gx_acc)
    loss_acc[...] = jnp.zeros_like(loss_acc)
    x = x_all[...]

    def tile(base):
        y = y_all[pl.ds(base, BM), :]
        score = lax.dot_general(y, x, NT, preferred_element_type=jnp.float32)
        rows = base + lax.broadcasted_iota(jnp.int32, (BM, NX), 0)
        paired = place[...] == rows
        z = score * slope + shift
        z = jnp.where(paired, -z, z)
        t = jnp.exp2(z)
        total = 1.0 + t
        weight = (jnp.where(paired, -scale, scale) * (t / total)).astype(jnp.bfloat16)
        small = t * (1.0 - t * (0.5 - t * (1.0 / 3.0)))
        loss = jnp.where(t < 2.0**-6, small, jnp.log(total))
        loss_acc[...] += jnp.sum(loss.reshape(BM // 8, 8, NX), axis=0)
        gx_acc[...] += lax.dot_general(weight, y, TN, preferred_element_type=jnp.float32)
        return jnp.dot(weight, x, preferred_element_type=jnp.float32)

    half = NY // 2 // BM

    def sib_step(i, carry):
        base = pl.multiple_of(i * BM, BM)
        gy_sib[pl.ds(base, BM), :] = tile(base + NY // 2).astype(jnp.bfloat16)
        return carry

    def own_step(i, carry):
        base = pl.multiple_of(i * BM, BM)
        gy_own[pl.ds(base, BM), :] = tile(base)
        return carry

    lax.fori_loop(0, half, sib_step, 0)
    lax.fori_loop(0, half, own_step, 0)
    gx_out[...] = gx_acc[...].astype(jnp.bfloat16)
    loss_ref[...] = jnp.broadcast_to(jnp.sum(loss_acc[...]), (8, 128))


def final_kernel(values_ref, own_ref, *refs):
    out_ref = refs[-1]
    unit, inverse = normalize(values_ref)
    grad = own_ref[...].astype(jnp.float32)
    for ref in refs[:-1]:
        grad = grad + ref[...].astype(jnp.float32)
    along = jnp.sum(grad * unit, axis=-1, keepdims=True)
    out_ref[...] = (grad - unit * along) * inverse


def finish(values, own, *parts):
    return pl.pallas_call(
        final_kernel,
        in_specs=[VMEM] * (2 + len(parts)),
        out_specs=VMEM,
        out_shape=jax.ShapeDtypeStruct((R, D), jnp.float32),
        name="unproject",
    )(values, own, *parts)


def f32(value):
    return value.astype(jnp.float32)


def local(images, texts, pair_index, log_scale, bias):
    row, col = lax.axis_index("row"), lax.axis_index("col")
    shard = pair_index // R
    codes = jnp.zeros((1, D), jnp.float32)
    codes = codes.at[0, :R].set(shard.astype(jnp.float32)).at[0, 256 : 256 + R].set((pair_index - shard * R).astype(jnp.float32))
    x_low, y_low = pl.pallas_call(
        prep_kernel,
        in_specs=[VMEM] * 3,
        out_specs=[VMEM] * 2,
        out_shape=[jax.ShapeDtypeStruct((RX, D), jnp.bfloat16), jax.ShapeDtypeStruct((R, D), jnp.bfloat16)],
        name="prep",
    )(images, texts, codes)

    x_z = send_col(x_low, dz=1)
    y_z = send_row(y_low, dz=1)
    xs = [x_low, x_z] + [send_col(v, dx=d) for d in (1, 3, 2) for v in (x_low, x_z)]
    ys = [y_low, y_z] + [send_row(v, dy=d) for d in (1, 3, 2) for v in (y_low, y_z)]
    xs = [xs[i] for i in (0, 1, 4, 5, 6, 7, 2, 3)]
    ys = [ys[i] for i in (0, 1, 4, 5, 6, 7, 2, 3)]
    ys = ys + [send_row(v, dc=1) for v in ys]

    scale = jnp.exp(log_scale[0])
    scalars = jnp.stack([scale * LOG2E, bias[0] * LOG2E, scale])
    at = jnp.stack([col, row // 4, (row // 2) % 2, row % 2]).astype(jnp.int32)
    gx, gy_own, gy_sib, loss = pl.pallas_call(
        score_kernel,
        in_specs=[SMEM] * 2 + [VMEM] * (N_COL + N_ROW),
        out_specs=[VMEM] * 4,
        out_shape=[
            jax.ShapeDtypeStruct((NX, D), jnp.bfloat16),
            jax.ShapeDtypeStruct((NY // 2, D), jnp.float32),
            jax.ShapeDtypeStruct((NY // 2, D), jnp.bfloat16),
            jax.ShapeDtypeStruct((8, 128), jnp.float32),
        ],
        scratch_shapes=[
            pltpu.VMEM((NX, D), jnp.bfloat16),
            pltpu.VMEM((NY, D), jnp.bfloat16),
            pltpu.VMEM((1, NX), jnp.int32),
            pltpu.VMEM((NX, D), jnp.float32),
            pltpu.VMEM((8, NX), jnp.float32),
        ],
        compiler_params=pltpu.CompilerParams(vmem_limit_bytes=60 << 20),
        cost_estimate=pl.CostEstimate(flops=6 * NX * NY * D, bytes_accessed=20 << 20, transcendentals=0),
        name="score",
    )(scalars, at, *xs, *ys)

    gy_core = send_row(gy_sib, dc=1)
    gx = [gx[k * R : (k + 1) * R] for k in range(N_COL)]
    gx_far = [send_col(gx[2 * d + 1], dx=d) for d in (1, 2, 3)]
    gx_near = [send_col(gx[2 * d], dx=d) for d in (1, 2, 3)]
    gx_z = sum((f32(v) for v in gx_far), f32(gx[1])).astype(jnp.bfloat16)
    gx_z = send_col(gx_z, dz=1)

    gy = [gy_own[k * R : (k + 1) * R] + f32(gy_core[k * R : (k + 1) * R]) for k in range(N_ROW // 2)]
    low = [v.astype(jnp.bfloat16) for v in gy]
    gy_far = [send_row(low[2 * d + 1], dy=d) for d in (1, 2, 3)]
    gy_near = [send_row(low[2 * d], dy=d) for d in (1, 2, 3)]
    gy_z = sum((f32(v) for v in gy_far), gy[1]).astype(jnp.bfloat16)
    gy_z = send_row(gy_z, dz=1)

    loss = loss + send_row(loss, dc=1)
    loss = loss + send_row(loss, dz=1)
    loss = loss + send_row(loss, dy=1) + send_row(loss, dy=2) + send_row(loss, dy=3)
    loss = loss + send_col(loss, dz=1)
    loss = loss + send_col(loss, dx=1) + send_col(loss, dx=2) + send_col(loss, dx=3)
    loss = loss[0, :1] / (R * N_ROW * N_COL)

    grad_x = finish(images, gx[0], *gx_near, gx_z)
    grad_y = finish(texts, gy[0], *gy_near, gy_z)
    return loss, grad_x, grad_y


def solution(mesh):
    return jax.shard_map(
        local,
        mesh=mesh,
        in_specs=(P(("row", "col"), None), P(("col", "row"), None), P(("row", "col")), P(), P()),
        out_specs=(P(), P(("row", "col"), None), P(("col", "row"), None)),
        check_vma=False,
    )
```

```python
import functools

import jax
import jax.numpy as jnp
from jax import lax
from jax.experimental import pallas as pl
from jax.experimental.pallas import tpu as pltpu
from jax.sharding import PartitionSpec as P

EPS = 1e-06
LOG2E = 1.4426950408889634
N_ROW = 16
N_COL = 8
R = 192
D = 768
RX = R + 16
NX = R * 8
NY = R * 8
BM = 768
NT = (((1,), (1,)), ((), ()))
TN = (((0,), (0,)), ((), ()))
VMEM = pl.BlockSpec(memory_space=pltpu.VMEM)
SMEM = pl.BlockSpec(memory_space=pltpu.SMEM)


def send(value, move):
    pairs = []
    for r in range(N_ROW):
        for c in range(N_COL):
            y, zl, k, zh, x = move(r // 4, (r // 2) % 2, r % 2, c // 4, c % 4)
            pairs.append((r * N_COL + c, (((y % 4) * 2 + zl % 2) * 2 + k % 2) * N_COL + (zh % 2) * 4 + x % 4))
    return lax.ppermute(value, ("row", "col"), pairs)


def send_x(value, d):
    return send(value, lambda y, zl, k, zh, x: (y, zl, k, zh, x + d))


def send_y(value, d):
    return send(value, lambda y, zl, k, zh, x: (y + d, zl, k, zh, x))


def send_core(value):
    return send(value, lambda y, zl, k, zh, x: (y, zl, 1 - k, zh, x))


def swap_image_z(value):
    return send(value, lambda y, zl, k, zh, x: (y, 1 - zl, k, zh, x))


def swap_text_z(value):
    return send(value, lambda y, zl, k, zh, x: (y, 1 - zl, k, 1 - zh, x))


def normalize(ref):
    wide = ref[...].astype(jnp.float32)
    inverse = lax.rsqrt(jnp.sum(wide * wide, axis=-1, keepdims=True) + EPS)
    return wide * inverse, inverse


def call(kernel, outs, *args, name, scalars=0, aliases=None, scratch=(), flops=0, vmem=4):
    return pl.pallas_call(
        kernel,
        in_specs=[SMEM] * scalars + [VMEM] * (len(args) - scalars),
        out_specs=[VMEM] * len(outs),
        out_shape=[jax.ShapeDtypeStruct(shape, dtype) for shape, dtype in outs],
        input_output_aliases=aliases or {},
        scratch_shapes=scratch,
        compiler_params=pltpu.CompilerParams(vmem_limit_bytes=vmem << 20),
        cost_estimate=pl.CostEstimate(flops=flops, bytes_accessed=4 << 20, transcendentals=0),
        name=name,
    )(*args)


def prep_kernel(images_ref, texts_ref, pair_ref, x_ref, y_ref):
    x_ref[:R, :] = normalize(images_ref)[0].astype(jnp.bfloat16)
    y_ref[...] = normalize(texts_ref)[0].astype(jnp.bfloat16)
    pair = pair_ref[...]
    shard = ((pair.astype(jnp.float32) + 0.5) * (1.0 / R)).astype(jnp.int32)
    x_ref[R:, :] = jnp.zeros((16, D), jnp.bfloat16)
    x_ref[R:, :R] = jnp.broadcast_to(shard.astype(jnp.float32), (16, R)).astype(jnp.bfloat16)
    x_ref[R:, 256 : 256 + R] = jnp.broadcast_to((pair - shard * R).astype(jnp.float32), (16, R)).astype(jnp.bfloat16)


def join_kernel(a_ref, b_ref, out_ref):
    rows = a_ref.shape[0]
    out_ref[:rows, :] = a_ref[...]
    out_ref[rows:, :] = b_ref[...]


def join(a, b):
    return call(join_kernel, [((2 * a.shape[0], D), jnp.bfloat16)], a, b, name="join")[0]


def pack_kernel(at_ref, *refs):
    xs, ys = refs[:5], refs[5:10]
    x_all, place, y_all = refs[10:]
    my_y, my_zl, my_k, my_zh, my_x = [at_ref[i] for i in range(5)]
    slot = 0
    for ref in xs:
        for i in range(ref.shape[0] // RX):
            here = slice(slot * R, slot * R + R)
            x_all[here, :] = ref[i * RX : i * RX + R, :]
            codes = ref[i * RX + R : i * RX + RX, :].astype(jnp.float32).astype(jnp.int32)[:1, :]
            shard, offset = codes[:, :R], codes[:, 256 : 256 + R]
            dz = (shard >> 6) ^ my_zh
            dy = (((shard >> 2) & 3) - my_y) & 3
            dk = (shard & 1) ^ my_k
            mine = (((shard >> 4) & 3) == my_x) & (dz == (((shard >> 1) & 1) ^ my_zl))
            step = jnp.where(dy == 2, 6, jnp.where(dy == 3, 4, dy * 2))
            place[:, here] = jnp.where(mine, (dk * 8 + step + dz) * R + offset, -1)
            slot += 1
    slot = 0
    for ref in ys:
        y_all[slot * R : slot * R + ref.shape[0], :] = ref[...]
        slot += ref.shape[0] // R


def score_kernel(first, sc_ref, x_all, y_all, place, loss_in, gy_out, weights, loss_ref, loss_acc):
    slope, shift, scale = sc_ref[0], sc_ref[1], sc_ref[2]
    loss_acc[...] = jnp.zeros_like(loss_acc)

    def step(i, carry):
        base = pl.multiple_of(i * BM, BM)
        here = pl.ds(base, BM)
        x = x_all[...]
        score = lax.dot_general(y_all[here, :], x, NT, preferred_element_type=jnp.float32)
        rows = first + base + lax.broadcasted_iota(jnp.int32, (BM, NX), 0)
        paired = place[...] == rows
        z = score * slope + shift
        z = jnp.where(paired, -z, z)
        t = jnp.exp2(z)
        total = 1.0 + t
        weight = (jnp.where(paired, -scale, scale) * (t / total)).astype(jnp.bfloat16)
        small = t * (1.0 - t * (0.5 - t * (1.0 / 3.0)))
        loss = jnp.where(t < 2.0**-6, small, jnp.log(total))
        loss_acc[...] += jnp.sum(loss.reshape(BM // 8, 8, NX), axis=0)
        weights[here, :] = weight
        gy_out[here, :] = jnp.dot(weight, x, preferred_element_type=jnp.float32).astype(gy_out.dtype)
        return carry

    lax.fori_loop(0, NY // BM, step, 0)
    loss = loss_in[...] + jnp.sum(loss_acc[...])
    loss_ref[...] = loss
    if gy_out.shape[0] > NY:
        gy_out[NY:, :] = jnp.zeros((16, D), gy_out.dtype)
        for i in range(3):
            part = loss.astype(jnp.bfloat16)
            gy_out[NY:, i * 128 : i * 128 + 128] = jnp.concatenate([part, part], axis=0)
            loss = loss - part.astype(jnp.float32)


def image_kernel(slots, w_own, w_sib, y_own, y_sib, *outs):
    outs = list(outs)
    for slot in slots:
        here = slice(slot * R, slot * R + 2 * R)
        grad = lax.dot_general(w_own[:, here], y_own[...], TN, preferred_element_type=jnp.float32)
        grad += lax.dot_general(w_sib[:, here], y_sib[...], TN, preferred_element_type=jnp.float32)
        at = 0
        while at < 2 * R:
            ref = outs.pop(0)
            ref[...] = grad[at : at + ref.shape[0], :].astype(ref.dtype)
            at += ref.shape[0]


def add_kernel(direct, sibling, loss, own, zed, plus, minus, two, two_z, loss_out):
    slot = 0
    for ref in (own, zed, plus, minus, two, two_z):
        here = slice(slot, slot + ref.shape[0])
        ref[...] = (direct[here, :] + sibling[here, :].astype(jnp.float32)).astype(ref.dtype)
        slot += ref.shape[0]
    total = loss[...]
    for i in range(3):
        total = total + sibling[NY : NY + 8, i * 128 : i * 128 + 128].astype(jnp.float32)
    loss_out[...] = total


F32, BF16 = jnp.float32, jnp.bfloat16
LOSS = ((8, 128), F32)
NEAR = [((R, D), F32), ((R, D), F32), ((2 * R, D), F32), ((2 * R, D), F32)]
AWAY = [((R, D), BF16), ((R, D), BF16)]


def turn_kernel(plus, minus, two, two_z, plus_out, minus_out):
    plus_out[:R, :] = (plus[:R, :] + two[...].astype(F32)).astype(BF16)
    plus_out[R:, :] = plus[R:, :].astype(BF16)
    minus_out[:R, :] = minus[:R, :].astype(BF16)
    minus_out[R:, :] = (minus[R:, :] + two_z[...].astype(F32)).astype(BF16)


def turn_loss_kernel(plus, minus, two, two_z, loss, plus_out, minus_out, loss_out):
    turn_kernel(plus, minus, two, two_z, plus_out, minus_out)
    loss_out[...] = loss[...]


def far_kernel(own, plus, minus, out):
    out[...] = (own[...] + plus[R:, :].astype(F32) + minus[R:, :].astype(F32)).astype(BF16)


def far_loss_kernel(own, plus, minus, loss, step, out, loss_out):
    far_kernel(own, plus, minus, out)
    loss_out[...] = loss[...] + step[...]


def final_kernel(values_ref, own_ref, plus, minus, zed, out_ref):
    unit, inverse = normalize(values_ref)
    grad = own_ref[...] + plus[:R, :].astype(F32) + minus[:R, :].astype(F32) + zed[...].astype(F32)
    along = jnp.sum(grad * unit, axis=-1, keepdims=True)
    out_ref[...] = (grad - unit * along) * inverse


def final_loss_kernel(values_ref, own_ref, plus, minus, zed, loss, step, out_ref, loss_out):
    final_kernel(values_ref, own_ref, plus, minus, zed, out_ref)
    loss_out[...] = (loss[...] + step[...]) * (1.0 / (R * N_ROW * N_COL))


def gather(own, swap, shift):
    zed = swap(own)
    two = shift(own, 2)
    both = join(own, zed)
    return [both, shift(both, -1), shift(both, 1), two, shift(zed, 2)]


def turn(near, away, shift, *loss):
    two, two_z = shift(away[0], 1), shift(away[1], -1)
    outs = [((2 * R, D), BF16)] * 2
    if loss:
        return call(turn_loss_kernel, outs + [LOSS], near[2], near[3], two, two_z, *loss, name="turn", vmem=8)
    return call(turn_kernel, outs, near[2], near[3], two, two_z, name="turn", vmem=8)


def far(near, plus, minus, swap, *loss):
    out = ((R, D), BF16)
    if loss:
        value, total = call(far_loss_kernel, [out, LOSS], near[1], plus, minus, *loss, name="far")
        return swap(value), total
    return swap(call(far_kernel, [out], near[1], plus, minus, name="far")[0])


def local(images, texts, pair_index, log_scale, bias):
    row, col = lax.axis_index("row"), lax.axis_index("col")
    x_low, y_low = call(
        prep_kernel,
        [((RX, D), jnp.bfloat16), ((R, D), jnp.bfloat16)],
        images, texts, pair_index.reshape(1, R),
        name="prep",
    )
    xs = gather(x_low, swap_image_z, send_x)
    ys = gather(y_low, swap_text_z, send_y)

    scale = jnp.exp(log_scale[0])
    scalars = jnp.stack([scale * LOG2E, bias[0] * LOG2E, scale])
    at = jnp.stack([row // 4, (row // 2) % 2, row % 2, col // 4, col % 4]).astype(jnp.int32)
    x_all, place, y_own = call(
        pack_kernel,
        [((NX, D), jnp.bfloat16), ((1, NX), jnp.int32), ((NY, D), jnp.bfloat16)],
        at, *xs, *ys,
        name="pack", scalars=1, vmem=12,
    )
    y_sib = send_core(y_own)
    flops = 4 * NX * NY * D

    def score(first, y_all, loss, out, name):
        return call(
            functools.partial(score_kernel, first),
            [out, ((NY, NX), BF16), LOSS],
            scalars, x_all, y_all, place, loss,
            name=name, scalars=1, flops=flops, vmem=30,
            scratch=[pltpu.VMEM((8, NX), F32)],
        )

    gy_own, w_own, loss = score(0, y_own, jnp.zeros((8, 128), F32), ((NY, D), F32), "score_own")
    gy_sib, w_sib, loss = score(NY, y_sib, loss, ((NY + 16, D), BF16), "score_sib")
    gy_core = send_core(gy_sib)
    weights = (w_own, w_sib, y_own, y_sib)
    gx_away = call(functools.partial(image_kernel, (6,)), AWAY, *weights, name="image_away", flops=flops // 8, vmem=16)
    *gy, loss = call(add_kernel, NEAR + AWAY + [LOSS], gy_own, gy_core, loss, name="add", vmem=16)
    gy_near, gy_away = gy[:4], gy[4:]

    gx_near = call(
        functools.partial(image_kernel, (0, 2, 4)), NEAR, *weights, name="image_near", flops=3 * flops // 8, vmem=16
    )
    gx_plus, gx_minus = turn(gx_near, gx_away, send_x)
    gy_plus, gy_minus, loss = turn(gy_near, gy_away, send_y, loss)
    gx_plus, gx_minus = send_x(gx_plus, 1), send_x(gx_minus, -1)
    gy_plus, gy_minus = send_y(gy_plus, 1), send_y(gy_minus, -1)

    loss = loss + swap_image_z(loss)
    loss = loss + swap_text_z(loss)
    step = send(loss, lambda y, zl, k, zh, x: (y, zl, k, zh, x ^ 1))
    gx_far, loss = far(gx_near, gx_plus, gx_minus, swap_image_z, loss, step)
    gy_far = far(gy_near, gy_plus, gy_minus, swap_text_z)
    loss = loss + send(loss, lambda y, zl, k, zh, x: (y, zl, k, zh, x ^ 2))
    loss = loss + send(loss, lambda y, zl, k, zh, x: (y ^ 1, zl, k, zh, x))
    step = send(loss, lambda y, zl, k, zh, x: (y ^ 2, zl, k, zh, x))

    grad = ((R, D), F32)
    grad_x = call(final_kernel, [grad], images, gx_near[0], gx_plus, gx_minus, gx_far, name="unproject")[0]
    grad_y, loss = call(
        final_loss_kernel, [grad, LOSS], texts, gy_near[0], gy_plus, gy_minus, gy_far, loss, step, name="unproject"
    )
    return loss[0, :1], grad_x, grad_y


def solution(mesh):
    return jax.shard_map(
        local,
        mesh=mesh,
        in_specs=(P(("row", "col"), None), P(("col", "row"), None), P(("row", "col")), P(), P()),
        out_specs=(P(), P(("row", "col"), None), P(("col", "row"), None)),
        check_vma=False,
    )
```

```python
import functools

import jax
import jax.numpy as jnp
from jax import lax
from jax.experimental import pallas as pl
from jax.experimental.pallas import tpu as pltpu
from jax.sharding import PartitionSpec as P

EPS = 1e-06
LOG2E = 1.4426950408889634
N_ROW = 16
N_COL = 8
R = 192
D = 768
RX = R + 16
NX = R * 8
NY = R * 8
FIRST = 4 * R
NEAR = 6 * R
NT = (((1,), (1,)), ((), ()))
TN = (((0,), (0,)), ((), ()))
F32, BF16 = jnp.float32, jnp.bfloat16
LOSS = ((8, 128), F32)
PARTS = [((R, D), F32), ((R, D), F32), ((2 * R, D), F32), ((2 * R, D), F32)]
AWAY = [((R, D), BF16), ((R, D), BF16)]
VMEM = pl.BlockSpec(memory_space=pltpu.VMEM)
SMEM = pl.BlockSpec(memory_space=pltpu.SMEM)


def send(value, move):
    pairs = []
    for r in range(N_ROW):
        for c in range(N_COL):
            y, zl, k, zh, x = move(r // 4, (r // 2) % 2, r % 2, c // 4, c % 4)
            pairs.append((r * N_COL + c, (((y % 4) * 2 + zl % 2) * 2 + k % 2) * N_COL + (zh % 2) * 4 + x % 4))
    return lax.ppermute(value, ("row", "col"), pairs)


def send_x(value, d):
    return send(value, lambda y, zl, k, zh, x: (y, zl, k, zh, x + d))


def send_y(value, d):
    return send(value, lambda y, zl, k, zh, x: (y + d, zl, k, zh, x))


def send_core(value):
    return send(value, lambda y, zl, k, zh, x: (y, zl, 1 - k, zh, x))


def swap_image_z(value):
    return send(value, lambda y, zl, k, zh, x: (y, 1 - zl, k, zh, x))


def swap_text_z(value):
    return send(value, lambda y, zl, k, zh, x: (y, 1 - zl, k, 1 - zh, x))


def normalize(ref):
    wide = ref[...].astype(jnp.float32)
    inverse = lax.rsqrt(jnp.sum(wide * wide, axis=-1, keepdims=True) + EPS)
    return wide * inverse, inverse


def call(kernel, outs, *args, name, scalars=0, aliases=None, scratch=(), flops=0, vmem=4, after=()):
    count = len(args)

    def body(*refs):
        kernel(*refs[:count], *refs[count + len(after) :])

    return pl.pallas_call(
        body,
        in_specs=[SMEM] * scalars + [VMEM] * (count - scalars + len(after)),
        out_specs=[VMEM] * len(outs),
        out_shape=[jax.ShapeDtypeStruct(shape, dtype) for shape, dtype in outs],
        input_output_aliases=aliases or {},
        scratch_shapes=scratch,
        compiler_params=pltpu.CompilerParams(vmem_limit_bytes=vmem << 20),
        cost_estimate=pl.CostEstimate(flops=flops, bytes_accessed=4 << 20, transcendentals=0),
        name=name,
    )(*args, *after)


def prep_kernel(log_scale_ref, bias_ref, images_hbm, texts_hbm, pair_hbm, x_ref, y_ref, const_ref, images, texts, pairs, sems):
    copies = [
        pltpu.make_async_copy(source, target, sems.at[i])
        for i, (source, target) in enumerate(((images_hbm, images), (texts_hbm, texts), (pair_hbm, pairs)))
    ]
    for copy in copies:
        copy.start()
    scale = jnp.exp(jnp.full((8, 128), log_scale_ref[0], F32))
    const_ref[:8, :] = scale * LOG2E
    const_ref[8:16, :] = jnp.full((8, 128), bias_ref[0] * LOG2E, F32)
    const_ref[16:, :] = scale
    for copy in copies:
        copy.wait()
    x_ref[:R, :] = normalize(images)[0].astype(BF16)
    y_ref[...] = normalize(texts)[0].astype(BF16)
    pair = pairs[...]
    shard = ((pair.astype(F32) + 0.5) * (1.0 / R)).astype(jnp.int32)
    x_ref[R:, :] = jnp.zeros((16, D), BF16)
    x_ref[R:, :R] = jnp.broadcast_to(shard.astype(F32), (16, R)).astype(BF16)
    x_ref[R:, 256 : 256 + R] = jnp.broadcast_to((pair - shard * R).astype(F32), (16, R)).astype(BF16)


def place_codes(codes):
    row, col = lax.axis_index("row"), lax.axis_index("col")
    my_y, my_zl, my_k, my_zh, my_x = row >> 2, (row >> 1) & 1, row & 1, col >> 2, col & 3
    codes = codes.astype(jnp.float32).astype(jnp.int32)[:1, :]
    shard, offset = codes[:, :R], codes[:, 256 : 256 + R]
    dz = (shard >> 6) ^ my_zh
    dy = (((shard >> 2) & 3) - my_y) & 3
    dk = (shard & 1) ^ my_k
    mine = (((shard >> 4) & 3) == my_x) & (dz == (((shard >> 1) & 1) ^ my_zl))
    slot = jnp.where(dy == 2, 6 + dz, jnp.where(dy == 0, dz, 2 * dz + jnp.where(dy == 1, 2, 3)))
    return jnp.where(mine, (dk * 8 + slot) * R + offset, -1)


def near_image_kernel(*refs):
    for i, ref in enumerate(refs[:6]):
        here = slice(i * R, (i + 1) * R)
        refs[6][here, :] = ref[:R, :]
        refs[7][:, here] = place_codes(ref[R:, :])


def text_kernel(first, *refs):
    slot = first
    for ref in refs[:-1]:
        if ref.shape[0] == R:
            refs[-1][slot * R : (slot + 1) * R, :] = ref[...]
            slot += 1


def gate_kernel(value, out):
    out[...] = value[...]


def gate(value, *after):
    return call(gate_kernel, [(value.shape, value.dtype)], value, name="gate", after=after)[0]


def away_image_kernel(x_in, place_in, two, two_z, out, place):
    place[...] = place_in[...]
    for slot, ref in ((6, two), (7, two_z)):
        here = slice(slot * R, (slot + 1) * R)
        out[here, :] = ref[:R, :]
        place[:, here] = place_codes(ref[R:, :])


def weigh(x, y, first, place, sc_ref):
    slope, shift, scale = sc_ref[0:1, 0:1], sc_ref[8:9, 0:1], sc_ref[16:17, 0:1]
    score = lax.dot_general(y, x, NT, preferred_element_type=jnp.float32)
    paired = place == first + lax.broadcasted_iota(jnp.int32, score.shape, 0)
    z = score * slope + shift
    z = jnp.where(paired, -z, z)
    t = jnp.exp2(z)
    total = 1.0 + t
    weight = (jnp.where(paired, -scale, scale) * (t / total)).astype(jnp.bfloat16)
    loss = jnp.where(t < 2.0**-8, t * (LOG2E - t * (0.5 * LOG2E)), jnp.log2(total))
    return weight, jnp.sum(loss.reshape(y.shape[0] // 8, 8, x.shape[0]), axis=0)


def score_first_kernel(consts, x_all, y_all, place, gy_out, weights, loss_ref):
    x = x_all[:NEAR, :]
    weight, loss = weigh(x, y_all[:FIRST, :], 0, place[:, :NEAR], consts)
    weights[:FIRST, :NEAR] = weight
    gy_out[:FIRST, :] = jnp.dot(weight, x, preferred_element_type=F32)
    loss_ref[...] = jnp.zeros((8, 128), F32) + jnp.sum(loss)


def score_second_kernel(consts, x_all, y_all, place, loss_in, gy_in, w_in, gy_out, weights, loss_ref):
    x = x_all[:NEAR, :]
    weight, loss = weigh(x, y_all[FIRST:NEAR, :], FIRST, place[:, :NEAR], consts)
    weights[FIRST:NEAR, :NEAR] = weight
    gy_out[FIRST:NEAR, :] = jnp.dot(weight, x, preferred_element_type=F32)
    loss_ref[...] = loss_in[...] + jnp.sum(loss)


def score_rest_kernel(consts, x_all, y_all, place, loss_in, gy_in, w_in, gy_out, weights, loss_ref):
    x = x_all[NEAR:, :]
    weight, loss = weigh(x, y_all[:NEAR, :], 0, place[:, NEAR:], consts)
    weights[:NEAR, NEAR:] = weight
    gy_out[:NEAR, :] = gy_in[:NEAR, :] + jnp.dot(weight, x, preferred_element_type=F32)
    total = jnp.sum(loss)
    x = x_all[...]
    weight, loss = weigh(x, y_all[NEAR:, :], NEAR, place[...], consts)
    weights[NEAR:, :] = weight
    gy_out[NEAR:, :] = jnp.dot(weight, x, preferred_element_type=F32)
    loss_ref[...] = loss_in[...] + total + jnp.sum(loss)


def score_sib_kernel(consts, x_all, y_all, place, loss_in, gy_out, weights, loss_ref, loss_acc):
    loss_acc[...] = jnp.zeros_like(loss_acc)

    def step(i, carry):
        base = pl.multiple_of(i * FIRST, FIRST)
        here = pl.ds(base, FIRST)
        x = x_all[...]
        weight, loss = weigh(x, y_all[here, :], NY + base, place[...], consts)
        loss_acc[...] += loss
        weights[here, :] = weight
        gy_out[here, :] = jnp.dot(weight, x, preferred_element_type=F32).astype(BF16)
        return carry

    lax.fori_loop(0, NY // FIRST, step, 0)
    loss = loss_in[...] + jnp.sum(loss_acc[...])
    loss_ref[...] = loss
    gy_out[NY:, :] = jnp.zeros((16, D), jnp.bfloat16)
    for i in range(3):
        part = loss.astype(jnp.bfloat16)
        gy_out[NY:, i * 128 : i * 128 + 128] = jnp.concatenate([part, part], axis=0)
        loss = loss - part.astype(jnp.float32)


def image_kernel(slots, w_own, w_sib, y_own, y_sib, *outs):
    outs = list(outs)
    for slot in slots:
        here = slice(slot * R, slot * R + 2 * R)
        grad = lax.dot_general(w_own[:, here], y_own[...], TN, preferred_element_type=F32)
        grad += lax.dot_general(w_sib[:, here], y_sib[...], TN, preferred_element_type=F32)
        at = 0
        while at < 2 * R:
            ref = outs.pop(0)
            ref[...] = grad[at : at + ref.shape[0], :].astype(ref.dtype)
            at += ref.shape[0]


def add_kernel(direct, sibling, loss, own, zed, plus, minus, two, two_z, loss_out):
    def part(slot):
        here = slice(slot * R, (slot + 1) * R)
        return direct[here, :] + sibling[here, :].astype(F32)

    own[...], zed[...] = part(0), part(1)
    plus[:R, :], plus[R:, :] = part(2), part(4)
    minus[:R, :], minus[R:, :] = part(3), part(5)
    two[...], two_z[...] = part(6).astype(BF16), part(7).astype(BF16)
    total = loss[...]
    for i in range(3):
        total = total + sibling[NY : NY + 8, i * 128 : i * 128 + 128].astype(jnp.float32)
    loss_out[...] = total


def turn_kernel(plus, minus, two, two_z, plus_out, minus_out):
    plus_out[:R, :] = (plus[:R, :] + two[...].astype(F32)).astype(BF16)
    plus_out[R:, :] = plus[R:, :].astype(BF16)
    minus_out[:R, :] = minus[:R, :].astype(BF16)
    minus_out[R:, :] = (minus[R:, :] + two_z[...].astype(F32)).astype(BF16)


def turn_loss_kernel(plus, minus, two, two_z, loss, plus_out, minus_out, loss_out):
    turn_kernel(plus, minus, two, two_z, plus_out, minus_out)
    loss_out[...] = loss[...]


def far_kernel(own, plus, minus, out):
    out[...] = (own[...] + plus[R:, :].astype(F32) + minus[R:, :].astype(F32)).astype(BF16)


def far_loss_kernel(own, plus, minus, loss, step, out, loss_out):
    far_kernel(own, plus, minus, out)
    loss_out[...] = loss[...] + step[...]


def final_kernel(values_ref, own_ref, plus, minus, zed, out_ref):
    unit, inverse = normalize(values_ref)
    grad = own_ref[...] + plus[:R, :].astype(F32) + minus[:R, :].astype(F32) + zed[...].astype(F32)
    along = jnp.sum(grad * unit, axis=-1, keepdims=True)
    out_ref[...] = (grad - unit * along) * inverse


def final_loss_kernel(values_ref, own_ref, plus, minus, zed, loss, step, out_ref, loss_out):
    final_kernel(values_ref, own_ref, plus, minus, zed, out_ref)
    loss_out[...] = (loss[...] + step[...]) * (1.0 / (LOG2E * R * N_ROW * N_COL))


def turn(near, away, shift, *loss):
    two, two_z = shift(away[0], 1), shift(away[1], -1)
    outs = [((2 * R, D), BF16)] * 2
    if loss:
        return call(turn_loss_kernel, outs + [LOSS], near[2], near[3], two, two_z, *loss, name="turn", vmem=8)
    return call(turn_kernel, outs, near[2], near[3], two, two_z, name="turn", vmem=8)


def far(near, plus, minus, swap, *loss):
    out = ((R, D), BF16)
    if loss:
        value, total = call(far_loss_kernel, [out, LOSS], near[1], plus, minus, *loss, name="far")
        return swap(value), total
    return swap(call(far_kernel, [out], near[1], plus, minus, name="far")[0])


def local(images, texts, pair_index, log_scale, bias):
    x_low, y_low, consts = pl.pallas_call(
        prep_kernel,
        in_specs=[SMEM] * 2 + [pl.BlockSpec(memory_space=pltpu.HBM)] * 3,
        out_specs=[VMEM] * 3,
        out_shape=[jax.ShapeDtypeStruct(*out) for out in (((RX, D), BF16), ((R, D), BF16), ((24, 128), F32))],
        scratch_shapes=[
            pltpu.VMEM((R, D), BF16),
            pltpu.VMEM((R, D), BF16),
            pltpu.VMEM((1, R), jnp.int32),
            pltpu.SemaphoreType.DMA((3,)),
        ],
        compiler_params=pltpu.CompilerParams(vmem_limit_bytes=56 << 20),
        name="prep",
    )(log_scale, bias, images, texts, pair_index.reshape(1, R))
    x_zed, y_zed = swap_image_z(x_low), swap_text_z(y_low)
    x_plus, x_minus = send_x(x_low, -1), send_x(x_low, 1)
    y_plus, y_minus = send_y(y_low, -1), send_y(y_low, 1)
    x_next = gate(x_zed, x_plus, x_minus)
    y_next = gate(y_zed, y_plus, y_minus, x_next)
    x_plus_z, x_minus_z = send_x(x_next, -1), send_x(x_next, 1)
    y_plus_z, y_minus_z = send_y(y_next, -1), send_y(y_next, 1)
    x_two, x_two_z = send_x(x_minus, 1), send_x(x_plus_z, -1)
    y_two, y_two_z = send_y(y_minus, 1), send_y(y_plus_z, -1)

    image_rows, places = ((NX, D), BF16), ((1, NX), jnp.int32)
    x_all, place = call(
        near_image_kernel, [image_rows, places], x_low, x_zed, x_plus, x_plus_z, x_minus, x_minus_z,
        name="near_images", vmem=8,
    )
    text_rows = ((NY, D), BF16)
    y_all = call(
        functools.partial(text_kernel, 0), [text_rows], y_low, y_zed, y_plus, y_minus,
        name="first_texts", after=(x_all, x_two),
    )[0]

    flops = 4 * NX * NY * D
    scored = [((NY, D), F32), ((NY, NX), BF16), LOSS]
    gy_own, w_own, loss = call(
        score_first_kernel, scored, consts, x_all, y_all, place, name="score_first", flops=flops * 3 // 8, vmem=24
    )
    y_all = call(
        functools.partial(text_kernel, 4), [text_rows], y_all, y_plus_z, y_minus_z,
        name="second_texts", aliases={0: 0}, after=(loss, x_two_z),
    )[0]
    gy_own, w_own, loss = call(
        score_second_kernel, scored, consts, x_all, y_all, place, loss, gy_own, w_own,
        name="score_second", flops=flops * 3 // 16, vmem=20, aliases={5: 0, 6: 1},
    )
    x_all, place = call(
        away_image_kernel, [image_rows, places], x_all, place, x_two, x_two_z,
        name="away_images", aliases={0: 0}, after=(loss,),
    )
    y_all = call(
        functools.partial(text_kernel, 6), [text_rows], y_all, y_two, y_two_z,
        name="away_texts", aliases={0: 0}, after=(loss,),
    )[0]
    s_all = send_core(y_all)
    gy_own, w_own, loss = call(
        score_rest_kernel, scored, consts, x_all, y_all, place, loss, gy_own, w_own,
        name="score_rest", flops=flops * 7 // 16, vmem=30, aliases={5: 0, 6: 1},
    )
    gy_sib, w_sib, loss = call(
        score_sib_kernel, [((NY + 16, D), BF16)] + scored[1:], consts, x_all, s_all, place, loss,
        name="score_sib", flops=flops, vmem=30, scratch=[pltpu.VMEM((8, NX), F32)],
    )
    gy_core = send_core(gy_sib)
    weights = (w_own, w_sib, y_all, s_all)
    gx_away = call(functools.partial(image_kernel, (6,)), AWAY, *weights, name="image_away", flops=flops // 8, vmem=16)
    *gy, loss = call(add_kernel, PARTS + AWAY + [LOSS], gy_own, gy_core, loss, name="add", vmem=16)
    gy_near, gy_away = gy[:4], gy[4:]

    gx_ring = call(
        functools.partial(image_kernel, (2, 4)), PARTS[2:], *weights, name="image_ring", flops=flops // 4, vmem=16
    )
    gx_near = call(
        functools.partial(image_kernel, (0,)), PARTS[:2], *weights, name="image_near", flops=flops // 8, vmem=16
    )
    gx_near = gx_near + gx_ring
    gx_plus, gx_minus = turn(gx_near, gx_away, send_x)
    gy_plus, gy_minus, loss = turn(gy_near, gy_away, send_y, loss)
    gx_plus, gx_minus = send_x(gx_plus, 1), send_x(gx_minus, -1)
    gy_plus, gy_minus = send_y(gy_plus, 1), send_y(gy_minus, -1)

    loss = loss + swap_image_z(loss)
    loss = loss + swap_text_z(loss)
    step = send(loss, lambda y, zl, k, zh, x: (y, zl, k, zh, x ^ 1))
    gx_far, loss = far(gx_near, gx_plus, gx_minus, swap_image_z, loss, step)
    gy_far = far(gy_near, gy_plus, gy_minus, swap_text_z)
    loss = loss + send(loss, lambda y, zl, k, zh, x: (y, zl, k, zh, x ^ 2))
    loss = loss + send(loss, lambda y, zl, k, zh, x: (y ^ 1, zl, k, zh, x))
    step = send(loss, lambda y, zl, k, zh, x: (y ^ 2, zl, k, zh, x))

    grad = ((R, D), F32)
    grad_x = call(final_kernel, [grad], images, gx_near[0], gx_plus, gx_minus, gx_far, name="unproject")[0]
    grad_y, loss = call(
        final_loss_kernel, [grad, LOSS], texts, gy_near[0], gy_plus, gy_minus, gy_far, loss, step, name="unproject"
    )
    return loss[0, :1], grad_x, grad_y


def solution(mesh):
    return jax.shard_map(
        local,
        mesh=mesh,
        in_specs=(P(("row", "col"), None), P(("col", "row"), None), P(("row", "col")), P(), P()),
        out_specs=(P(), P(("row", "col"), None), P(("col", "row"), None)),
        check_vma=False,
    )
```

```python
import functools

import jax
import jax.numpy as jnp
from jax import lax
from jax.experimental import pallas as pl
from jax.experimental.pallas import tpu as pltpu
from jax.sharding import PartitionSpec as P

EPS = 1e-06
LOG2E = 1.4426950408889634
N_ROW = 16
N_COL = 8
R = 192
D = 768
RX = R + 16
NX = R * 8
NY = R * 8
FIRST = 4 * R
NEAR = 6 * R
NT = (((1,), (1,)), ((), ()))
TN = (((0,), (0,)), ((), ()))
F32, BF16 = jnp.float32, jnp.bfloat16
LOSS = ((8, 128), F32)
PARTS = [((R, D), F32), ((R, D), F32), ((2 * R, D), F32), ((2 * R, D), F32)]
AWAY = [((R, D), BF16), ((R, D), BF16)]
VMEM = pl.BlockSpec(memory_space=pltpu.VMEM)
SMEM = pl.BlockSpec(memory_space=pltpu.SMEM)


def send(value, move):
    pairs = []
    for r in range(N_ROW):
        for c in range(N_COL):
            y, zl, k, zh, x = move(r // 4, (r // 2) % 2, r % 2, c // 4, c % 4)
            pairs.append((r * N_COL + c, (((y % 4) * 2 + zl % 2) * 2 + k % 2) * N_COL + (zh % 2) * 4 + x % 4))
    return lax.ppermute(value, ("row", "col"), pairs)


def send_x(value, d):
    return send(value, lambda y, zl, k, zh, x: (y, zl, k, zh, x + d))


def send_y(value, d):
    return send(value, lambda y, zl, k, zh, x: (y + d, zl, k, zh, x))


def send_core(value):
    return send(value, lambda y, zl, k, zh, x: (y, zl, 1 - k, zh, x))


def swap_image_z(value):
    return send(value, lambda y, zl, k, zh, x: (y, 1 - zl, k, zh, x))


def swap_text_z(value):
    return send(value, lambda y, zl, k, zh, x: (y, 1 - zl, k, 1 - zh, x))


def normalize(ref):
    wide = ref[...].astype(jnp.float32)
    inverse = lax.rsqrt(jnp.sum(wide * wide, axis=-1, keepdims=True) + EPS)
    return wide * inverse, inverse


def call(kernel, outs, *args, name, scalars=0, aliases=None, scratch=(), flops=0, vmem=4, after=()):
    count = len(args)

    def body(*refs):
        kernel(*refs[:count], *refs[count + len(after) :])

    return pl.pallas_call(
        body,
        in_specs=[SMEM] * scalars + [VMEM] * (count - scalars + len(after)),
        out_specs=[VMEM] * len(outs),
        out_shape=[jax.ShapeDtypeStruct(shape, dtype) for shape, dtype in outs],
        input_output_aliases=aliases or {},
        scratch_shapes=scratch,
        compiler_params=pltpu.CompilerParams(vmem_limit_bytes=vmem << 20),
        cost_estimate=pl.CostEstimate(flops=flops, bytes_accessed=4 << 20, transcendentals=0),
        name=name,
    )(*args, *after)


def prep_kernel(log_scale_ref, bias_ref, images_hbm, texts_hbm, pair_hbm, x_ref, y_ref, const_ref, images, texts, pairs, sems):
    copies = [
        pltpu.make_async_copy(source, target, sems.at[i])
        for i, (source, target) in enumerate(((images_hbm, images), (texts_hbm, texts), (pair_hbm, pairs)))
    ]
    for copy in copies:
        copy.start()
    scale = jnp.exp(jnp.full((8, 128), log_scale_ref[0], F32))
    const_ref[:8, :] = scale * LOG2E
    const_ref[8:16, :] = jnp.full((8, 128), bias_ref[0] * LOG2E, F32)
    const_ref[16:, :] = scale
    for copy in copies:
        copy.wait()
    x_ref[:R, :] = normalize(images)[0].astype(BF16)
    y_ref[...] = normalize(texts)[0].astype(BF16)
    pair = pairs[...]
    shard = ((pair.astype(F32) + 0.5) * (1.0 / R)).astype(jnp.int32)
    x_ref[R:, :] = jnp.zeros((16, D), BF16)
    x_ref[R:, :R] = jnp.broadcast_to(shard.astype(F32), (16, R)).astype(BF16)
    x_ref[R:, 256 : 256 + R] = jnp.broadcast_to((pair - shard * R).astype(F32), (16, R)).astype(BF16)


def place_codes(codes):
    row, col = lax.axis_index("row"), lax.axis_index("col")
    my_y, my_zl, my_k, my_zh, my_x = row >> 2, (row >> 1) & 1, row & 1, col >> 2, col & 3
    codes = codes.astype(jnp.float32).astype(jnp.int32)[:1, :]
    shard, offset = codes[:, :R], codes[:, 256 : 256 + R]
    dz = (shard >> 6) ^ my_zh
    dy = (((shard >> 2) & 3) - my_y) & 3
    dk = (shard & 1) ^ my_k
    mine = (((shard >> 4) & 3) == my_x) & (dz == (((shard >> 1) & 1) ^ my_zl))
    slot = jnp.where(dy == 2, 6 + dz, jnp.where(dy == 0, dz, 2 * dz + jnp.where(dy == 1, 2, 3)))
    return jnp.where(mine, (dk * 8 + slot) * R + offset, -1)


def near_image_kernel(*refs):
    for i, ref in enumerate(refs[:6]):
        here = slice(i * R, (i + 1) * R)
        refs[6][here, :] = ref[:R, :]
        refs[7][:, here] = place_codes(ref[R:, :])


def text_kernel(first, *refs):
    slot = first
    for ref in refs[:-1]:
        if ref.shape[0] == R:
            refs[-1][slot * R : (slot + 1) * R, :] = ref[...]
            slot += 1


def gate_kernel(value, out):
    out[...] = value[...]


def gate(value, *after):
    return call(gate_kernel, [(value.shape, value.dtype)], value, name="gate", after=after)[0]


def away_image_kernel(x_in, place_in, two, two_z, out, place):
    place[...] = place_in[...]
    for slot, ref in ((6, two), (7, two_z)):
        here = slice(slot * R, (slot + 1) * R)
        out[here, :] = ref[:R, :]
        place[:, here] = place_codes(ref[R:, :])


def weigh(x, y, first, place, sc_ref):
    slope, shift, scale = sc_ref[0:1, 0:1], sc_ref[8:9, 0:1], sc_ref[16:17, 0:1]
    score = lax.dot_general(y, x, NT, preferred_element_type=jnp.float32)
    paired = place == first + lax.broadcasted_iota(jnp.int32, score.shape, 0)
    z = score * slope + shift
    z = jnp.where(paired, -z, z)
    t = jnp.exp2(z)
    total = 1.0 + t
    weight = (jnp.where(paired, -scale, scale) * (t / total)).astype(jnp.bfloat16)
    loss = jnp.where(t < 2.0**-8, t * (LOG2E - t * (0.5 * LOG2E)), jnp.log2(total))
    return weight, jnp.sum(loss.reshape(y.shape[0] // 8, 8, x.shape[0]), axis=0)


def score_first_kernel(consts, x_all, y_all, place, gy_out, weights, loss_ref):
    x = x_all[:NEAR, :]
    weight, loss = weigh(x, y_all[:FIRST, :], 0, place[:, :NEAR], consts)
    weights[:FIRST, :NEAR] = weight
    gy_out[:FIRST, :] = jnp.dot(weight, x, preferred_element_type=F32)
    loss_ref[...] = jnp.zeros((8, 128), F32) + jnp.sum(loss)


def score_second_kernel(consts, x_all, y_all, place, loss_in, gy_in, w_in, gy_out, weights, loss_ref):
    x = x_all[:NEAR, :]
    weight, loss = weigh(x, y_all[FIRST:NEAR, :], FIRST, place[:, :NEAR], consts)
    weights[FIRST:NEAR, :NEAR] = weight
    gy_out[FIRST:NEAR, :] = jnp.dot(weight, x, preferred_element_type=F32)
    loss_ref[...] = loss_in[...] + jnp.sum(loss)


def score_rest_kernel(consts, x_all, y_all, place, loss_in, gy_in, w_in, gy_out, weights, loss_ref):
    x = x_all[NEAR:, :]
    weight, loss = weigh(x, y_all[:NEAR, :], 0, place[:, NEAR:], consts)
    weights[:NEAR, NEAR:] = weight
    gy_out[:NEAR, :] = gy_in[:NEAR, :] + jnp.dot(weight, x, preferred_element_type=F32)
    total = jnp.sum(loss)
    x = x_all[...]
    weight, loss = weigh(x, y_all[NEAR:, :], NEAR, place[...], consts)
    weights[NEAR:, :] = weight
    gy_out[NEAR:, :] = jnp.dot(weight, x, preferred_element_type=F32)
    loss_ref[...] = loss_in[...] + total + jnp.sum(loss)


def score_sib_kernel(consts, x_all, y_all, place, loss_in, gy_out, weights, loss_ref, loss_acc):
    loss_acc[...] = jnp.zeros_like(loss_acc)

    def step(i, carry):
        base = pl.multiple_of(i * FIRST, FIRST)
        here = pl.ds(base, FIRST)
        x = x_all[...]
        weight, loss = weigh(x, y_all[here, :], NY + base, place[...], consts)
        loss_acc[...] += loss
        weights[here, :] = weight
        gy_out[here, :] = jnp.dot(weight, x, preferred_element_type=F32).astype(BF16)
        return carry

    lax.fori_loop(0, NY // FIRST, step, 0)
    loss = loss_in[...] + jnp.sum(loss_acc[...])
    loss_ref[...] = loss
    write_loss(loss, gy_out, NY)


def write_loss(loss, ref, row):
    ref[row:, :] = jnp.zeros((16, D), BF16)
    for i in range(3):
        part = loss.astype(BF16)
        ref[row:, i * 128 : i * 128 + 128] = jnp.concatenate([part, part], axis=0)
        loss = loss - part.astype(F32)


def read_loss(ref, row):
    parts = [ref[row:, i * 128 : i * 128 + 128].astype(F32) for i in range(3)]
    return (parts[0] + parts[1] + parts[2])[:8, :]


def image_kernel(slots, w_own, w_sib, y_own, y_sib, *outs):
    outs = list(outs)
    for slot in slots:
        here = slice(slot * R, slot * R + 2 * R)
        grad = lax.dot_general(w_own[:, here], y_own[...], TN, preferred_element_type=F32)
        grad += lax.dot_general(w_sib[:, here], y_sib[...], TN, preferred_element_type=F32)
        at = 0
        while at < 2 * R:
            ref = outs.pop(0)
            ref[...] = grad[at : at + ref.shape[0], :].astype(ref.dtype)
            at += ref.shape[0]


def add_kernel(direct, sibling, loss, own, zed, plus, minus, two, two_z, loss_out):
    def part(slot):
        here = slice(slot * R, (slot + 1) * R)
        return direct[here, :] + sibling[here, :].astype(F32)

    own[...], zed[...] = part(0), part(1)
    plus[:R, :], plus[R:, :] = part(2), part(4)
    minus[:R, :], minus[R:, :] = part(3), part(5)
    total = loss[...] + read_loss(sibling, NY)
    for slot, ref in ((6, two), (7, two_z)):
        ref[:R, :] = part(slot).astype(BF16)
        write_loss(total, ref, R)
    loss_out[...] = total


def turn_kernel(plus, minus, two, two_z, plus_out, minus_out):
    plus_out[:R, :] = (plus[:R, :] + two[:R, :].astype(F32)).astype(BF16)
    plus_out[R:, :] = plus[R:, :].astype(BF16)
    minus_out[:R, :] = minus[:R, :].astype(BF16)
    minus_out[R:, :] = (minus[R:, :] + two_z[:R, :].astype(F32)).astype(BF16)


def turn_loss_kernel(plus, minus, two, two_z, loss, plus_out, minus_out, loss_out):
    turn_kernel(plus, minus, two, two_z, plus_out, minus_out)
    odd = (lax.axis_index("row") >> 2) & 1
    loss_out[...] = loss[...] + jnp.where(odd == 1, read_loss(two, R), read_loss(two_z, R))


def far_kernel(own, plus, minus, out):
    out[...] = (own[...] + plus[R:, :].astype(F32) + minus[R:, :].astype(F32)).astype(BF16)


def far_loss_kernel(own, plus, minus, loss, step, out, loss_out):
    far_kernel(own, plus, minus, out)
    loss_out[...] = loss[...] + step[...]


def final_kernel(values_ref, own_ref, plus, minus, zed, out_ref):
    unit, inverse = normalize(values_ref)
    grad = own_ref[...] + plus[:R, :].astype(F32) + minus[:R, :].astype(F32) + zed[...].astype(F32)
    along = jnp.sum(grad * unit, axis=-1, keepdims=True)
    out_ref[...] = (grad - unit * along) * inverse


def final_loss_kernel(values_ref, own_ref, plus, minus, zed, loss, step, out_ref, loss_out):
    final_kernel(values_ref, own_ref, plus, minus, zed, out_ref)
    loss_out[0] = (loss[0, 0] + step[0, 0]) * (1.0 / (LOG2E * R * N_ROW * N_COL))


def turn(near, away, shift, loss=(), after=(), flops=0):
    two, two_z = shift(away[0], 1), shift(away[1], -1)
    outs = [((2 * R, D), BF16)] * 2
    if loss:
        return call(
            turn_loss_kernel, outs + [LOSS], near[2], near[3], two, two_z, *loss, name="turn", vmem=8, after=after
        )
    return call(turn_kernel, outs, near[2], near[3], two, two_z, name="turn", vmem=8, flops=flops)


def far(near, plus, minus, swap, *loss):
    out = ((R, D), BF16)
    if loss:
        value, total = call(far_loss_kernel, [out, LOSS], near[1], plus, minus, *loss, name="far")
        return swap(value), total
    return swap(call(far_kernel, [out], near[1], plus, minus, name="far")[0])


def local(images, texts, pair_index, log_scale, bias):
    x_low, y_low, consts = pl.pallas_call(
        prep_kernel,
        in_specs=[SMEM] * 2 + [pl.BlockSpec(memory_space=pltpu.HBM)] * 3,
        out_specs=[VMEM] * 3,
        out_shape=[jax.ShapeDtypeStruct(*out) for out in (((RX, D), BF16), ((R, D), BF16), ((24, 128), F32))],
        scratch_shapes=[
            pltpu.VMEM((R, D), BF16),
            pltpu.VMEM((R, D), BF16),
            pltpu.VMEM((1, R), jnp.int32),
            pltpu.SemaphoreType.DMA((3,)),
        ],
        compiler_params=pltpu.CompilerParams(vmem_limit_bytes=56 << 20),
        name="prep",
    )(log_scale, bias, images, texts, pair_index.reshape(1, R))
    x_zed, y_zed = swap_image_z(x_low), swap_text_z(y_low)
    x_plus, x_minus = send_x(x_low, -1), send_x(x_low, 1)
    y_plus, y_minus = send_y(y_low, -1), send_y(y_low, 1)
    x_next = gate(x_zed, x_plus, x_minus)
    y_next = gate(y_zed, y_plus, y_minus, x_next)
    x_plus_z, x_minus_z = send_x(x_next, -1), send_x(x_next, 1)
    y_plus_z, y_minus_z = send_y(y_next, -1), send_y(y_next, 1)
    x_two, x_two_z = send_x(x_minus, 1), send_x(x_plus_z, -1)
    y_two, y_two_z = send_y(y_minus, 1), send_y(y_plus_z, -1)

    image_rows, places = ((NX, D), BF16), ((1, NX), jnp.int32)
    x_all, place = call(
        near_image_kernel, [image_rows, places], x_low, x_zed, x_plus, x_plus_z, x_minus, x_minus_z,
        name="near_images", vmem=8,
    )
    text_rows = ((NY, D), BF16)
    y_all = call(
        functools.partial(text_kernel, 0), [text_rows], y_low, y_zed, y_plus, y_minus,
        name="first_texts", after=(x_all, x_two),
    )[0]

    flops = 4 * NX * NY * D
    scored = [((NY, D), F32), ((NY, NX), BF16), LOSS]
    gy_own, w_own, loss = call(
        score_first_kernel, scored, consts, x_all, y_all, place, name="score_first", flops=flops * 3 // 8, vmem=24
    )
    y_all = call(
        functools.partial(text_kernel, 4), [text_rows], y_all, y_plus_z, y_minus_z,
        name="second_texts", aliases={0: 0}, after=(loss, x_two_z),
    )[0]
    gy_own, w_own, loss = call(
        score_second_kernel, scored, consts, x_all, y_all, place, loss, gy_own, w_own,
        name="score_second", flops=flops * 3 // 16, vmem=20, aliases={5: 0, 6: 1},
    )
    x_all, place = call(
        away_image_kernel, [image_rows, places], x_all, place, x_two, x_two_z,
        name="away_images", aliases={0: 0}, after=(loss,),
    )
    y_all = call(
        functools.partial(text_kernel, 6), [text_rows], y_all, y_two, y_two_z,
        name="away_texts", aliases={0: 0}, after=(loss,),
    )[0]
    s_all = send_core(y_all)
    gy_own, w_own, loss = call(
        score_rest_kernel, scored, consts, x_all, y_all, place, loss, gy_own, w_own,
        name="score_rest", flops=flops * 7 // 16, vmem=30, aliases={5: 0, 6: 1},
    )
    gy_sib, w_sib, loss = call(
        score_sib_kernel, [((NY + 16, D), BF16)] + scored[1:], consts, x_all, s_all, place, loss,
        name="score_sib", flops=flops, vmem=30, scratch=[pltpu.VMEM((8, NX), F32)],
    )
    gy_core = send_core(gy_sib)
    weights = (w_own, w_sib, y_all, s_all)
    gx_away = call(functools.partial(image_kernel, (6,)), AWAY, *weights, name="image_away", flops=flops // 8, vmem=16)
    *gy, loss = call(add_kernel, PARTS + [((R + 16, D), BF16)] * 2 + [LOSS], gy_own, gy_core, loss, after=gx_away, name="add", vmem=16)
    gy_near, gy_away = gy[:4], gy[4:]

    gx_ring = call(
        functools.partial(image_kernel, (2, 4)), PARTS[2:], *weights, name="image_ring", flops=flops // 4, vmem=16
    )
    gx_near = call(
        functools.partial(image_kernel, (0,)), PARTS[:2], *weights, name="image_near", flops=flops // 8, vmem=16
    )
    gx_near = gx_near + gx_ring
    gx_plus, gx_minus = turn(gx_near, gx_away, send_x, flops=flops // 4)
    gy_plus, gy_minus, loss = turn(gy_near, gy_away, send_y, (loss,), after=(gx_plus,))
    gx_plus, gx_minus = send_x(gx_plus, 1), send_x(gx_minus, -1)
    gy_plus, gy_minus = send_y(gy_plus, 1), send_y(gy_minus, -1)

    loss = loss + swap_image_z(loss)
    loss = loss + swap_text_z(loss)
    step = send(loss, lambda y, zl, k, zh, x: (y, zl, k, zh, x ^ 1))
    gx_far, loss = far(gx_near, gx_plus, gx_minus, swap_image_z, loss, step)
    gy_far = far(gy_near, gy_plus, gy_minus, swap_text_z)
    loss = loss + send(loss, lambda y, zl, k, zh, x: (y, zl, k, zh, x ^ 2))
    step = send(loss, lambda y, zl, k, zh, x: (y ^ 2, zl, k, zh, x))

    grad = ((R, D), F32)
    grad_x = call(final_kernel, [grad], images, gx_near[0], gx_plus, gx_minus, gx_far, name="unproject")[0]
    grad_y, loss = pl.pallas_call(
        final_loss_kernel,
        in_specs=[VMEM] * 7,
        out_specs=[VMEM, SMEM],
        out_shape=[jax.ShapeDtypeStruct((R, D), F32), jax.ShapeDtypeStruct((1,), F32)],
        compiler_params=pltpu.CompilerParams(vmem_limit_bytes=8 << 20),
        name="unproject",
    )(texts, gy_near[0], gy_plus, gy_minus, gy_far, loss, step)
    return loss, grad_x, grad_y


def solution(mesh):
    return jax.shard_map(
        local,
        mesh=mesh,
        in_specs=(P(("row", "col"), None), P(("col", "row"), None), P(("row", "col")), P(), P()),
        out_specs=(P(), P(("row", "col"), None), P(("col", "row"), None)),
        check_vma=False,
    )
```

```python
import functools

import jax
import jax.numpy as jnp
from jax import lax
from jax.experimental import pallas as pl
from jax.experimental.pallas import tpu as pltpu
from jax.sharding import PartitionSpec as P

EPS = 1e-06
LOG2E = 1.4426950408889634
N_ROW = 16
N_COL = 8
R = 192
D = 768
RX = R + 16
NX = R * 8
NY = R * 8
FIRST = 4 * R
NEAR = 6 * R
NT = (((1,), (1,)), ((), ()))
TN = (((0,), (0,)), ((), ()))
F32, BF16 = jnp.float32, jnp.bfloat16
LOSS = ((8, 128), F32)
PARTS = [((R, D), F32), ((R, D), F32), ((2 * R, D), F32), ((2 * R, D), F32)]
AWAY = [((R, D), BF16), ((R, D), BF16)]
VMEM = pl.BlockSpec(memory_space=pltpu.VMEM)
SMEM = pl.BlockSpec(memory_space=pltpu.SMEM)


def send(value, move):
    pairs = []
    for r in range(N_ROW):
        for c in range(N_COL):
            y, zl, k, zh, x = move(r // 4, (r // 2) % 2, r % 2, c // 4, c % 4)
            pairs.append((r * N_COL + c, (((y % 4) * 2 + zl % 2) * 2 + k % 2) * N_COL + (zh % 2) * 4 + x % 4))
    return lax.ppermute(value, ("row", "col"), pairs)


def send_x(value, d):
    return send(value, lambda y, zl, k, zh, x: (y, zl, k, zh, x + d))


def send_y(value, d):
    return send(value, lambda y, zl, k, zh, x: (y + d, zl, k, zh, x))


def send_core(value):
    return send(value, lambda y, zl, k, zh, x: (y, zl, 1 - k, zh, x))


def swap_image_z(value):
    return send(value, lambda y, zl, k, zh, x: (y, 1 - zl, k, zh, x))


def swap_text_z(value):
    return send(value, lambda y, zl, k, zh, x: (y, 1 - zl, k, 1 - zh, x))


def normalize(ref):
    wide = ref[...].astype(jnp.float32)
    inverse = lax.rsqrt(jnp.sum(wide * wide, axis=-1, keepdims=True) + EPS)
    return wide * inverse, inverse


def call(kernel, outs, *args, name, scalars=0, aliases=None, scratch=(), flops=0, vmem=4, after=()):
    count = len(args)

    def body(*refs):
        kernel(*refs[:count], *refs[count + len(after) :])

    return pl.pallas_call(
        body,
        in_specs=[SMEM] * scalars + [VMEM] * (count - scalars + len(after)),
        out_specs=[VMEM] * len(outs),
        out_shape=[jax.ShapeDtypeStruct(shape, dtype) for shape, dtype in outs],
        input_output_aliases=aliases or {},
        scratch_shapes=scratch,
        compiler_params=pltpu.CompilerParams(vmem_limit_bytes=vmem << 20),
        cost_estimate=pl.CostEstimate(flops=flops, bytes_accessed=4 << 20, transcendentals=0),
        name=name,
    )(*args, *after)


def prep_text_kernel(texts_ref, y_ref):
    y_ref[...] = normalize(texts_ref)[0].astype(BF16)


def prep_image_kernel(log_scale_ref, bias_ref, images_ref, pair_ref, x_ref, const_ref):
    scale = jnp.exp(jnp.full((8, 128), log_scale_ref[0], F32))
    const_ref[:8, :] = scale * LOG2E
    const_ref[8:16, :] = jnp.full((8, 128), bias_ref[0] * LOG2E, F32)
    const_ref[16:, :] = scale
    x_ref[:R, :] = normalize(images_ref)[0].astype(BF16)
    pair = pair_ref[...]
    shard = ((pair.astype(F32) + 0.5) * (1.0 / R)).astype(jnp.int32)
    x_ref[R:, :] = jnp.zeros((16, D), BF16)
    x_ref[R:, :R] = jnp.broadcast_to(shard.astype(F32), (16, R)).astype(BF16)
    x_ref[R:, 256 : 256 + R] = jnp.broadcast_to((pair - shard * R).astype(F32), (16, R)).astype(BF16)


def place_codes(codes):
    row, col = lax.axis_index("row"), lax.axis_index("col")
    my_y, my_zl, my_k, my_zh, my_x = row >> 2, (row >> 1) & 1, row & 1, col >> 2, col & 3
    codes = codes.astype(jnp.float32).astype(jnp.int32)[:1, :]
    shard, offset = codes[:, :R], codes[:, 256 : 256 + R]
    dz = (shard >> 6) ^ my_zh
    dy = (((shard >> 2) & 3) - my_y) & 3
    dk = (shard & 1) ^ my_k
    mine = (((shard >> 4) & 3) == my_x) & (dz == (((shard >> 1) & 1) ^ my_zl))
    slot = jnp.where(dy == 2, 6 + dz, jnp.where(dy == 0, dz, 2 * dz + jnp.where(dy == 1, 2, 3)))
    return jnp.where(mine, (dk * 8 + slot) * R + offset, -1)


def near_image_kernel(*refs):
    for i, ref in enumerate(refs[:6]):
        here = slice(i * R, (i + 1) * R)
        refs[6][here, :] = ref[:R, :]
        refs[7][:, here] = place_codes(ref[R:, :])


def text_kernel(first, *refs):
    slot = first
    for ref in refs[:-1]:
        if ref.shape[0] == R:
            refs[-1][slot * R : (slot + 1) * R, :] = ref[...]
            slot += 1


def gate_kernel(value, out):
    out[...] = value[...]


def gate(value, *after):
    return call(gate_kernel, [(value.shape, value.dtype)], value, name="gate", after=after)[0]


def away_image_kernel(x_in, place_in, two, two_z, out, place):
    place[...] = place_in[...]
    for slot, ref in ((6, two), (7, two_z)):
        here = slice(slot * R, (slot + 1) * R)
        out[here, :] = ref[:R, :]
        place[:, here] = place_codes(ref[R:, :])


def weigh(x, y, first, place, sc_ref):
    slope, shift, scale = sc_ref[0:1, 0:1], sc_ref[8:9, 0:1], sc_ref[16:17, 0:1]
    score = lax.dot_general(y, x, NT, preferred_element_type=jnp.float32)
    paired = place == first + lax.broadcasted_iota(jnp.int32, score.shape, 0)
    z = score * slope + shift
    z = jnp.where(paired, -z, z)
    t = jnp.exp2(z)
    total = 1.0 + t
    weight = (jnp.where(paired, -scale, scale) * (t / total)).astype(jnp.bfloat16)
    loss = jnp.where(t < 2.0**-8, t * (LOG2E - t * (0.5 * LOG2E)), jnp.log2(total))
    return weight, jnp.sum(loss.reshape(y.shape[0] // 8, 8, x.shape[0]), axis=0)


def score_first_kernel(consts, x_all, y_all, place, gy_out, weights, loss_ref):
    x = x_all[:NEAR, :]
    weight, loss = weigh(x, y_all[:FIRST, :], 0, place[:, :NEAR], consts)
    weights[:FIRST, :NEAR] = weight
    gy_out[:FIRST, :] = jnp.dot(weight, x, preferred_element_type=F32)
    loss_ref[...] = jnp.zeros((8, 128), F32) + jnp.sum(loss)


def score_second_kernel(consts, x_all, y_all, place, loss_in, gy_in, w_in, gy_out, weights, loss_ref):
    x = x_all[:NEAR, :]
    weight, loss = weigh(x, y_all[FIRST:NEAR, :], FIRST, place[:, :NEAR], consts)
    weights[FIRST:NEAR, :NEAR] = weight
    gy_out[FIRST:NEAR, :] = jnp.dot(weight, x, preferred_element_type=F32)
    loss_ref[...] = loss_in[...] + jnp.sum(loss)


def score_rest_kernel(consts, x_all, y_all, place, loss_in, gy_in, w_in, gy_out, weights, loss_ref):
    x = x_all[NEAR:, :]
    weight, loss = weigh(x, y_all[:NEAR, :], 0, place[:, NEAR:], consts)
    weights[:NEAR, NEAR:] = weight
    gy_out[:NEAR, :] = gy_in[:NEAR, :] + jnp.dot(weight, x, preferred_element_type=F32)
    total = jnp.sum(loss)
    x = x_all[...]
    weight, loss = weigh(x, y_all[NEAR:, :], NEAR, place[...], consts)
    weights[NEAR:, :] = weight
    gy_out[NEAR:, :] = jnp.dot(weight, x, preferred_element_type=F32)
    loss_ref[...] = loss_in[...] + total + jnp.sum(loss)


def score_sib_kernel(consts, x_all, y_all, place, loss_in, gy_out, weights, loss_ref, loss_acc):
    loss_acc[...] = jnp.zeros_like(loss_acc)

    def step(i, carry):
        base = pl.multiple_of(i * FIRST, FIRST)
        here = pl.ds(base, FIRST)
        x = x_all[...]
        weight, loss = weigh(x, y_all[here, :], NY + base, place[...], consts)
        loss_acc[...] += loss
        weights[here, :] = weight
        gy_out[here, :] = jnp.dot(weight, x, preferred_element_type=F32).astype(BF16)
        return carry

    lax.fori_loop(0, NY // FIRST, step, 0)
    loss = loss_in[...] + jnp.sum(loss_acc[...])
    loss_ref[...] = loss
    write_loss(loss, gy_out, NY)


def write_loss(loss, ref, row):
    ref[row:, :] = jnp.zeros((16, D), BF16)
    for i in range(3):
        part = loss.astype(BF16)
        ref[row:, i * 128 : i * 128 + 128] = jnp.concatenate([part, part], axis=0)
        loss = loss - part.astype(F32)


def read_loss(ref, row):
    parts = [ref[row:, i * 128 : i * 128 + 128].astype(F32) for i in range(3)]
    return (parts[0] + parts[1] + parts[2])[:8, :]


def image_kernel(slots, w_own, w_sib, y_own, y_sib, *outs):
    outs = list(outs)
    for slot in slots:
        here = slice(slot * R, slot * R + 2 * R)
        grad = lax.dot_general(w_own[:, here], y_own[...], TN, preferred_element_type=F32)
        grad += lax.dot_general(w_sib[:, here], y_sib[...], TN, preferred_element_type=F32)
        at = 0
        while at < 2 * R:
            ref = outs.pop(0)
            ref[...] = grad[at : at + ref.shape[0], :].astype(ref.dtype)
            at += ref.shape[0]


def add_kernel(direct, sibling, loss, own, zed, plus, minus, two, two_z, loss_out):
    def part(slot):
        here = slice(slot * R, (slot + 1) * R)
        return direct[here, :] + sibling[here, :].astype(F32)

    own[...], zed[...] = part(0), part(1)
    plus[:R, :], plus[R:, :] = part(2), part(4)
    minus[:R, :], minus[R:, :] = part(3), part(5)
    total = loss[...] + read_loss(sibling, NY)
    for slot, ref in ((6, two), (7, two_z)):
        ref[:R, :] = part(slot).astype(BF16)
        write_loss(total, ref, R)
    loss_out[...] = total


def turn_kernel(plus, minus, two, two_z, plus_out, minus_out):
    plus_out[:R, :] = (plus[:R, :] + two[:R, :].astype(F32)).astype(BF16)
    plus_out[R:, :] = plus[R:, :].astype(BF16)
    minus_out[:R, :] = minus[:R, :].astype(BF16)
    minus_out[R:, :] = (minus[R:, :] + two_z[:R, :].astype(F32)).astype(BF16)


def turn_loss_kernel(plus, minus, two, two_z, loss, plus_out, minus_out, loss_out):
    turn_kernel(plus, minus, two, two_z, plus_out, minus_out)
    odd = (lax.axis_index("row") >> 2) & 1
    loss_out[...] = loss[...] + jnp.where(odd == 1, read_loss(two, R), read_loss(two_z, R))


def far_kernel(own, plus, minus, out):
    out[...] = (own[...] + plus[R:, :].astype(F32) + minus[R:, :].astype(F32)).astype(BF16)


def far_loss_kernel(own, plus, minus, loss, step, out, loss_out):
    far_kernel(own, plus, minus, out)
    loss_out[...] = loss[...] + step[...]


def final_kernel(values_ref, own_ref, plus, minus, zed, out_ref):
    unit, inverse = normalize(values_ref)
    grad = own_ref[...] + plus[:R, :].astype(F32) + minus[:R, :].astype(F32) + zed[...].astype(F32)
    along = jnp.sum(grad * unit, axis=-1, keepdims=True)
    out_ref[...] = (grad - unit * along) * inverse


def final_loss_kernel(values_ref, own_ref, plus, minus, zed, loss, step, out_ref, loss_out):
    final_kernel(values_ref, own_ref, plus, minus, zed, out_ref)
    loss_out[0] = (loss[0, 0] + step[0, 0]) * (1.0 / (LOG2E * R * N_ROW * N_COL))


def turn(near, away, shift, loss=(), after=(), flops=0):
    two, two_z = shift(away[0], 1), shift(away[1], -1)
    outs = [((2 * R, D), BF16)] * 2
    if loss:
        return call(
            turn_loss_kernel, outs + [LOSS], near[2], near[3], two, two_z, *loss, name="turn", vmem=8, after=after
        )
    return call(turn_kernel, outs, near[2], near[3], two, two_z, name="turn", vmem=8, flops=flops)


def far(near, plus, minus, swap, *loss):
    out = ((R, D), BF16)
    if loss:
        value, total = call(far_loss_kernel, [out, LOSS], near[1], plus, minus, *loss, name="far")
        return swap(value), total
    return swap(call(far_kernel, [out], near[1], plus, minus, name="far")[0])


def local(images, texts, pair_index, log_scale, bias):
    x_low, consts = call(
        prep_image_kernel, [((RX, D), BF16), ((24, 128), F32)], log_scale, bias, images, pair_index.reshape(1, R),
        name="prep_images", scalars=2,
    )
    y_low = call(prep_text_kernel, [((R, D), BF16)], texts, name="prep_texts")[0]
    x_zed, y_zed = swap_image_z(x_low), swap_text_z(y_low)
    x_plus, x_minus = send_x(x_low, -1), send_x(x_low, 1)
    y_plus, y_minus = send_y(y_low, -1), send_y(y_low, 1)
    x_next = gate(x_zed, x_plus, x_minus)
    y_next = gate(gate(y_zed, y_plus), y_minus, x_next)
    x_plus_z, x_minus_z = send_x(x_next, -1), send_x(x_next, 1)
    y_plus_z, y_minus_z = send_y(y_next, -1), send_y(y_next, 1)
    x_two, x_two_z = send_x(x_minus, 1), send_x(x_plus_z, -1)
    y_two, y_two_z = send_y(y_minus, 1), send_y(y_plus_z, -1)

    image_rows, places = ((NX, D), BF16), ((1, NX), jnp.int32)
    x_all, place = call(
        near_image_kernel, [image_rows, places], x_low, x_zed, x_plus, x_plus_z, x_minus, x_minus_z,
        name="near_images", vmem=8,
    )
    text_rows = ((NY, D), BF16)
    y_all = call(
        functools.partial(text_kernel, 0), [text_rows], y_low, y_zed, y_plus, y_minus,
        name="first_texts", after=(x_all, x_two),
    )[0]

    flops = 4 * NX * NY * D
    scored = [((NY, D), F32), ((NY, NX), BF16), LOSS]
    gy_own, w_own, loss = call(
        score_first_kernel, scored, consts, x_all, y_all, place, name="score_first", flops=flops * 3 // 8, vmem=24
    )
    y_all = call(
        functools.partial(text_kernel, 4), [text_rows], y_all, y_plus_z, y_minus_z,
        name="second_texts", aliases={0: 0}, after=(loss, x_two_z),
    )[0]
    gy_own, w_own, loss = call(
        score_second_kernel, scored, consts, x_all, y_all, place, loss, gy_own, w_own,
        name="score_second", flops=flops * 3 // 16, vmem=20, aliases={5: 0, 6: 1},
    )
    x_all, place = call(
        away_image_kernel, [image_rows, places], x_all, place, x_two, x_two_z,
        name="away_images", aliases={0: 0}, after=(loss,),
    )
    y_all = call(
        functools.partial(text_kernel, 6), [text_rows], y_all, y_two, y_two_z,
        name="away_texts", aliases={0: 0}, after=(loss,),
    )[0]
    s_all = send_core(y_all)
    gy_own, w_own, loss = call(
        score_rest_kernel, scored, consts, x_all, y_all, place, loss, gy_own, w_own,
        name="score_rest", flops=flops * 7 // 16, vmem=30, aliases={5: 0, 6: 1},
    )
    gy_sib, w_sib, loss = call(
        score_sib_kernel, [((NY + 16, D), BF16)] + scored[1:], consts, x_all, s_all, place, loss,
        name="score_sib", flops=flops, vmem=30, scratch=[pltpu.VMEM((8, NX), F32)],
    )
    gy_core = send_core(gy_sib)
    weights = (w_own, w_sib, y_all, s_all)
    gx_away = call(functools.partial(image_kernel, (6,)), AWAY, *weights, name="image_away", flops=flops // 8, vmem=16)
    *gy, loss = call(add_kernel, PARTS + [((R + 16, D), BF16)] * 2 + [LOSS], gy_own, gy_core, loss, after=gx_away, name="add", vmem=16)
    gy_near, gy_away = gy[:4], gy[4:]

    gx_ring = call(
        functools.partial(image_kernel, (2, 4)), PARTS[2:], *weights, name="image_ring", flops=flops // 4, vmem=16
    )
    gx_near = call(
        functools.partial(image_kernel, (0,)), PARTS[:2], *weights, name="image_near", flops=flops // 8, vmem=16
    )
    gx_near = gx_near + gx_ring
    gx_plus, gx_minus = turn(gx_near, gx_away, send_x, flops=flops // 4)
    gy_plus, gy_minus, loss = turn(gy_near, gy_away, send_y, (loss,), after=(gx_plus,))
    gx_plus, gx_minus = send_x(gx_plus, 1), send_x(gx_minus, -1)
    gy_plus, gy_minus = send_y(gy_plus, 1), send_y(gy_minus, -1)

    loss = loss + swap_image_z(loss)
    loss = loss + swap_text_z(loss)
    step = send(loss, lambda y, zl, k, zh, x: (y, zl, k, zh, x ^ 1))
    gx_far, loss = far(gx_near, gx_plus, gx_minus, swap_image_z, loss, step)
    gy_far = far(gy_near, gy_plus, gy_minus, swap_text_z)
    loss = loss + send(loss, lambda y, zl, k, zh, x: (y, zl, k, zh, x ^ 2))
    step = send(loss, lambda y, zl, k, zh, x: (y ^ 2, zl, k, zh, x))

    grad = ((R, D), F32)
    grad_x = call(final_kernel, [grad], images, gx_near[0], gx_plus, gx_minus, gx_far, name="unproject")[0]
    grad_y, loss = pl.pallas_call(
        final_loss_kernel,
        in_specs=[VMEM] * 7,
        out_specs=[VMEM, SMEM],
        out_shape=[jax.ShapeDtypeStruct((R, D), F32), jax.ShapeDtypeStruct((1,), F32)],
        compiler_params=pltpu.CompilerParams(vmem_limit_bytes=8 << 20),
        name="unproject",
    )(texts, gy_near[0], gy_plus, gy_minus, gy_far, loss, step)
    return loss, grad_x, grad_y


def solution(mesh):
    return jax.shard_map(
        local,
        mesh=mesh,
        in_specs=(P(("row", "col"), None), P(("col", "row"), None), P(("row", "col")), P(), P()),
        out_specs=(P(), P(("row", "col"), None), P(("col", "row"), None)),
        check_vma=False,
    )
```

```python
import functools

import jax
import jax.numpy as jnp
from jax import lax
from jax.experimental import pallas as pl
from jax.experimental.pallas import tpu as pltpu
from jax.sharding import PartitionSpec as P

EPS = 1e-06
LOG2E = 1.4426950408889634
N_ROW = 16
N_COL = 8
R = 192
D = 768
RX = R + 16
NX = R * 8
NY = R * 8
FIRST = 4 * R
NEAR = 6 * R
NT = (((1,), (1,)), ((), ()))
TN = (((0,), (0,)), ((), ()))
F32, BF16 = jnp.float32, jnp.bfloat16
LOSS = ((8, 128), F32)
PARTS = [((R, D), F32), ((R, D), F32), ((2 * R, D), F32), ((2 * R, D), F32)]
AWAY = [((R, D), BF16), ((R, D), BF16)]
VMEM = pl.BlockSpec(memory_space=pltpu.VMEM)
SMEM = pl.BlockSpec(memory_space=pltpu.SMEM)


def send(value, move):
    pairs = []
    for r in range(N_ROW):
        for c in range(N_COL):
            y, zl, k, zh, x = move(r // 4, (r // 2) % 2, r % 2, c // 4, c % 4)
            pairs.append((r * N_COL + c, (((y % 4) * 2 + zl % 2) * 2 + k % 2) * N_COL + (zh % 2) * 4 + x % 4))
    return lax.ppermute(value, ("row", "col"), pairs)


def send_x(value, d):
    return send(value, lambda y, zl, k, zh, x: (y, zl, k, zh, x + d))


def send_y(value, d):
    return send(value, lambda y, zl, k, zh, x: (y + d, zl, k, zh, x))


def send_core(value):
    return send(value, lambda y, zl, k, zh, x: (y, zl, 1 - k, zh, x))


def swap_image_z(value):
    return send(value, lambda y, zl, k, zh, x: (y, 1 - zl, k, zh, x))


def swap_text_z(value):
    return send(value, lambda y, zl, k, zh, x: (y, 1 - zl, k, 1 - zh, x))


def normalize(ref):
    wide = ref[...].astype(jnp.float32)
    inverse = lax.rsqrt(jnp.sum(wide * wide, axis=-1, keepdims=True) + EPS)
    return wide * inverse, inverse


def call(kernel, outs, *args, name, scalars=0, aliases=None, scratch=(), flops=0, vmem=4, after=()):
    count = len(args)

    def body(*refs):
        kernel(*refs[:count], *refs[count + len(after) :])

    return pl.pallas_call(
        body,
        in_specs=[SMEM] * scalars + [VMEM] * (count - scalars + len(after)),
        out_specs=[VMEM] * len(outs),
        out_shape=[jax.ShapeDtypeStruct(shape, dtype) for shape, dtype in outs],
        input_output_aliases=aliases or {},
        scratch_shapes=scratch,
        compiler_params=pltpu.CompilerParams(vmem_limit_bytes=vmem << 20),
        cost_estimate=pl.CostEstimate(flops=flops, bytes_accessed=4 << 20, transcendentals=0),
        name=name,
    )(*args, *after)


def prep_text_kernel(texts_ref, y_ref):
    y_ref[...] = normalize(texts_ref)[0].astype(BF16)


def prep_image_kernel(log_scale_ref, bias_ref, images_ref, pair_ref, x_ref, const_ref):
    scale = jnp.exp(jnp.full((8, 128), log_scale_ref[0], F32))
    const_ref[:8, :] = scale * LOG2E
    const_ref[8:16, :] = jnp.full((8, 128), bias_ref[0] * LOG2E, F32)
    const_ref[16:, :] = scale
    x_ref[:R, :] = normalize(images_ref)[0].astype(BF16)
    pair = pair_ref[...]
    shard = ((pair.astype(F32) + 0.5) * (1.0 / R)).astype(jnp.int32)
    x_ref[R:, :] = jnp.zeros((16, D), BF16)
    x_ref[R:, :R] = jnp.broadcast_to(shard.astype(F32), (16, R)).astype(BF16)
    x_ref[R:, 256 : 256 + R] = jnp.broadcast_to((pair - shard * R).astype(F32), (16, R)).astype(BF16)


def place_codes(codes):
    row, col = lax.axis_index("row"), lax.axis_index("col")
    my_y, my_zl, my_k, my_zh, my_x = row >> 2, (row >> 1) & 1, row & 1, col >> 2, col & 3
    codes = codes.astype(jnp.float32).astype(jnp.int32)[:1, :]
    shard, offset = codes[:, :R], codes[:, 256 : 256 + R]
    dz = (shard >> 6) ^ my_zh
    dy = (((shard >> 2) & 3) - my_y) & 3
    dk = (shard & 1) ^ my_k
    mine = (((shard >> 4) & 3) == my_x) & (dz == (((shard >> 1) & 1) ^ my_zl))
    slot = jnp.where(dy == 2, 6 + dz, jnp.where(dy == 0, dz, 2 * dz + jnp.where(dy == 1, 2, 3)))
    return jnp.where(mine, (dk * 8 + slot) * R + offset, -1)


def near_image_kernel(*refs):
    for i, ref in enumerate(refs[:6]):
        here = slice(i * R, (i + 1) * R)
        refs[6][here, :] = ref[:R, :]
        refs[7][:, here] = place_codes(ref[R:, :])


def text_kernel(first, *refs):
    slot = first
    for ref in refs[:-1]:
        if ref.shape[0] == R:
            refs[-1][slot * R : (slot + 1) * R, :] = ref[...]
            slot += 1


def gate_kernel(value, out):
    out[...] = value[...]


def gate(value, *after):
    return call(gate_kernel, [(value.shape, value.dtype)], value, name="gate", after=after)[0]


def away_image_kernel(x_in, place_in, two, two_z, out, place):
    place[...] = place_in[...]
    for slot, ref in ((6, two), (7, two_z)):
        here = slice(slot * R, (slot + 1) * R)
        out[here, :] = ref[:R, :]
        place[:, here] = place_codes(ref[R:, :])


def weigh(x, y, first, place, sc_ref):
    slope, shift, scale = sc_ref[0:1, 0:1], sc_ref[8:9, 0:1], sc_ref[16:17, 0:1]
    score = lax.dot_general(y, x, NT, preferred_element_type=jnp.float32)
    paired = place == first + lax.broadcasted_iota(jnp.int32, score.shape, 0)
    z = score * slope + shift
    z = jnp.where(paired, -z, z)
    t = jnp.exp2(z)
    total = 1.0 + t
    weight = (jnp.where(paired, -scale, scale) * (t / total)).astype(jnp.bfloat16)
    loss = jnp.where(t < 2.0**-8, t * (LOG2E - t * (0.5 * LOG2E)), jnp.log2(total))
    return weight, jnp.sum(loss.reshape(y.shape[0] // 8, 8, x.shape[0]), axis=0)


def score_first_kernel(consts, x_all, y_all, place, gy_out, weights, loss_ref):
    x = x_all[:NEAR, :]
    weight, loss = weigh(x, y_all[:FIRST, :], 0, place[:, :NEAR], consts)
    weights[:FIRST, :NEAR] = weight
    gy_out[:FIRST, :] = jnp.dot(weight, x, preferred_element_type=F32)
    loss_ref[...] = jnp.zeros((8, 128), F32) + jnp.sum(loss)


def score_second_kernel(consts, x_all, y_all, place, loss_in, gy_in, w_in, gy_out, weights, loss_ref):
    x = x_all[:NEAR, :]
    weight, loss = weigh(x, y_all[FIRST:NEAR, :], FIRST, place[:, :NEAR], consts)
    weights[FIRST:NEAR, :NEAR] = weight
    gy_out[FIRST:NEAR, :] = jnp.dot(weight, x, preferred_element_type=F32)
    loss_ref[...] = loss_in[...] + jnp.sum(loss)


def score_rest_kernel(consts, x_all, y_all, place, loss_in, gy_in, w_in, gy_out, weights, loss_ref):
    x = x_all[NEAR:, :]
    weight, loss = weigh(x, y_all[:NEAR, :], 0, place[:, NEAR:], consts)
    weights[:NEAR, NEAR:] = weight
    gy_out[:NEAR, :] = gy_in[:NEAR, :] + jnp.dot(weight, x, preferred_element_type=F32)
    total = jnp.sum(loss)
    x = x_all[...]
    weight, loss = weigh(x, y_all[NEAR:, :], NEAR, place[...], consts)
    weights[NEAR:, :] = weight
    gy_out[NEAR:, :] = jnp.dot(weight, x, preferred_element_type=F32)
    loss_ref[...] = loss_in[...] + total + jnp.sum(loss)


def score_sib_kernel(consts, x_all, y_all, place, loss_in, gy_out, weights, loss_ref, loss_acc):
    loss_acc[...] = jnp.zeros_like(loss_acc)

    def step(i, carry):
        base = pl.multiple_of(i * FIRST, FIRST)
        here = pl.ds(base, FIRST)
        x = x_all[...]
        weight, loss = weigh(x, y_all[here, :], NY + base, place[...], consts)
        loss_acc[...] += loss
        weights[here, :] = weight
        gy_out[here, :] = jnp.dot(weight, x, preferred_element_type=F32).astype(BF16)
        return carry

    lax.fori_loop(0, NY // FIRST, step, 0)
    loss = loss_in[...] + jnp.sum(loss_acc[...])
    loss_ref[...] = loss
    write_loss(loss, gy_out, NY)


def write_loss(loss, ref, row):
    ref[row:, :] = jnp.zeros((16, D), BF16)
    for i in range(3):
        part = loss.astype(BF16)
        ref[row:, i * 128 : i * 128 + 128] = jnp.concatenate([part, part], axis=0)
        loss = loss - part.astype(F32)


def read_loss(ref, row):
    parts = [ref[row:, i * 128 : i * 128 + 128].astype(F32) for i in range(3)]
    return (parts[0] + parts[1] + parts[2])[:8, :]


def image_kernel(slots, w_own, w_sib, y_own, y_sib, *outs):
    outs = list(outs)
    for slot in slots:
        here = slice(slot * R, slot * R + 2 * R)
        grad = lax.dot_general(w_own[:, here], y_own[...], TN, preferred_element_type=F32)
        grad += lax.dot_general(w_sib[:, here], y_sib[...], TN, preferred_element_type=F32)
        at = 0
        while at < 2 * R:
            ref = outs.pop(0)
            ref[...] = grad[at : at + ref.shape[0], :].astype(ref.dtype)
            at += ref.shape[0]


def add_kernel(direct, sibling, loss, own, zed, plus, minus, two, two_z, loss_out):
    def part(slot):
        here = slice(slot * R, (slot + 1) * R)
        return direct[here, :] + sibling[here, :].astype(F32)

    own[...], zed[...] = part(0), part(1)
    plus[:R, :], plus[R:, :] = part(2), part(4)
    minus[:R, :], minus[R:, :] = part(3), part(5)
    total = loss[...] + read_loss(sibling, NY)
    for slot, ref in ((6, two), (7, two_z)):
        ref[:R, :] = part(slot).astype(BF16)
        write_loss(total, ref, R)
    loss_out[...] = total


def turn_kernel(plus, minus, two, two_z, plus_out, minus_out):
    plus_out[:R, :] = (plus[:R, :] + two[:R, :].astype(F32)).astype(BF16)
    plus_out[R:, :] = plus[R:, :].astype(BF16)
    minus_out[:R, :] = minus[:R, :].astype(BF16)
    minus_out[R:, :] = (minus[R:, :] + two_z[:R, :].astype(F32)).astype(BF16)


def turn_loss_kernel(plus, minus, two, two_z, loss, plus_out, minus_out, loss_out):
    turn_kernel(plus, minus, two, two_z, plus_out, minus_out)
    odd = (lax.axis_index("row") >> 2) & 1
    loss_out[...] = loss[...] + jnp.where(odd == 1, read_loss(two, R), read_loss(two_z, R))


def far_kernel(own, plus, minus, out):
    out[...] = (own[...] + plus[R:, :].astype(F32) + minus[R:, :].astype(F32)).astype(BF16)


def far_loss_kernel(own, plus, minus, loss, step, out, loss_out):
    far_kernel(own, plus, minus, out)
    loss_out[...] = loss[...] + step[...]


def final_kernel(values_ref, own_ref, plus, minus, zed, out_ref):
    unit, inverse = normalize(values_ref)
    grad = own_ref[...] + plus[:R, :].astype(F32) + minus[:R, :].astype(F32) + zed[...].astype(F32)
    along = jnp.sum(grad * unit, axis=-1, keepdims=True)
    out_ref[...] = (grad - unit * along) * inverse


def loss_kernel(loss, step, grad_x, grad_y, loss_out):
    loss_out[0] = (loss[0, 0] + step[0, 0]) * (1.0 / (LOG2E * R * N_ROW * N_COL))


def turn(near, away, shift, loss=(), after=(), flops=0):
    two, two_z = shift(away[0], 1), shift(away[1], -1)
    outs = [((2 * R, D), BF16)] * 2
    if loss:
        return call(
            turn_loss_kernel, outs + [LOSS], near[2], near[3], two, two_z, *loss, name="turn", vmem=8, after=after
        )
    return call(turn_kernel, outs, near[2], near[3], two, two_z, name="turn", vmem=8, flops=flops)


def far(near, plus, minus, swap, *loss):
    out = ((R, D), BF16)
    if loss:
        value, total = call(far_loss_kernel, [out, LOSS], near[1], plus, minus, *loss, name="far")
        return swap(value), total
    return swap(call(far_kernel, [out], near[1], plus, minus, name="far")[0])


def local(images, texts, pair_index, log_scale, bias):
    x_low, consts = call(
        prep_image_kernel, [((RX, D), BF16), ((24, 128), F32)], log_scale, bias, images, pair_index.reshape(1, R),
        name="prep_images", scalars=2,
    )
    y_low = call(prep_text_kernel, [((R, D), BF16)], texts, name="prep_texts")[0]
    x_zed, y_zed = swap_image_z(x_low), swap_text_z(y_low)
    x_plus, x_minus = send_x(x_low, -1), send_x(x_low, 1)
    y_plus, y_minus = send_y(y_low, -1), send_y(y_low, 1)
    x_next = gate(x_zed, x_plus, x_minus)
    y_next = gate(gate(y_zed, y_plus), y_minus, x_next)
    x_plus_z, x_minus_z = send_x(x_next, -1), send_x(x_next, 1)
    y_plus_z, y_minus_z = send_y(y_next, -1), send_y(y_next, 1)
    x_two, x_two_z = send_x(x_minus, 1), send_x(x_plus_z, -1)
    y_two, y_two_z = send_y(y_minus, 1), send_y(y_plus_z, -1)

    image_rows, places = ((NX, D), BF16), ((1, NX), jnp.int32)
    x_all, place = call(
        near_image_kernel, [image_rows, places], x_low, x_zed, x_plus, x_plus_z, x_minus, x_minus_z,
        name="near_images", vmem=8,
    )
    text_rows = ((NY, D), BF16)
    y_all = call(
        functools.partial(text_kernel, 0), [text_rows], y_low, y_zed, y_plus, y_minus,
        name="first_texts", after=(x_all, x_two),
    )[0]

    flops = 4 * NX * NY * D
    scored = [((NY, D), F32), ((NY, NX), BF16), LOSS]
    gy_own, w_own, loss = call(
        score_first_kernel, scored, consts, x_all, y_all, place, name="score_first", flops=flops * 3 // 8, vmem=24
    )
    y_all = call(
        functools.partial(text_kernel, 4), [text_rows], y_all, y_plus_z, y_minus_z,
        name="second_texts", aliases={0: 0}, after=(loss, x_two_z),
    )[0]
    gy_own, w_own, loss = call(
        score_second_kernel, scored, consts, x_all, y_all, place, loss, gy_own, w_own,
        name="score_second", flops=flops * 3 // 16, vmem=20, aliases={5: 0, 6: 1},
    )
    x_all, place = call(
        away_image_kernel, [image_rows, places], x_all, place, x_two, x_two_z,
        name="away_images", aliases={0: 0}, after=(loss,),
    )
    y_all = call(
        functools.partial(text_kernel, 6), [text_rows], y_all, y_two, y_two_z,
        name="away_texts", aliases={0: 0}, after=(loss,),
    )[0]
    s_all = send_core(y_all)
    gy_own, w_own, loss = call(
        score_rest_kernel, scored, consts, x_all, y_all, place, loss, gy_own, w_own,
        name="score_rest", flops=flops * 7 // 16, vmem=30, aliases={5: 0, 6: 1},
    )
    gy_sib, w_sib, loss = call(
        score_sib_kernel, [((NY + 16, D), BF16)] + scored[1:], consts, x_all, s_all, place, loss,
        name="score_sib", flops=flops, vmem=30, scratch=[pltpu.VMEM((8, NX), F32)],
    )
    gy_core = send_core(gy_sib)
    weights = (w_own, w_sib, y_all, s_all)
    gx_away = call(functools.partial(image_kernel, (6,)), AWAY, *weights, name="image_away", flops=flops // 8, vmem=16)
    *gy, loss = call(add_kernel, PARTS + [((R + 16, D), BF16)] * 2 + [LOSS], gy_own, gy_core, loss, after=gx_away, name="add", vmem=16)
    gy_near, gy_away = gy[:4], gy[4:]

    gx_ring = call(
        functools.partial(image_kernel, (2, 4)), PARTS[2:], *weights, name="image_ring", flops=flops // 4, vmem=16
    )
    gx_near = call(
        functools.partial(image_kernel, (0,)), PARTS[:2], *weights, name="image_near", flops=flops // 8, vmem=16
    )
    gx_near = gx_near + gx_ring
    gx_plus, gx_minus = turn(gx_near, gx_away, send_x, flops=flops // 4)
    gy_plus, gy_minus, loss = turn(gy_near, gy_away, send_y, (loss,), after=(gx_plus,))
    gx_plus, gx_minus = send_x(gx_plus, 1), send_x(gx_minus, -1)
    gy_plus, gy_minus = send_y(gy_plus, 1), send_y(gy_minus, -1)

    loss = loss + swap_image_z(loss)
    loss = loss + swap_text_z(loss)
    step = send(loss, lambda y, zl, k, zh, x: (y, zl, k, zh, x ^ 1))
    gx_far, loss = far(gx_near, gx_plus, gx_minus, swap_image_z, loss, step)
    gy_far = far(gy_near, gy_plus, gy_minus, swap_text_z)
    loss = loss + send(loss, lambda y, zl, k, zh, x: (y, zl, k, zh, x ^ 2))
    step = send(loss, lambda y, zl, k, zh, x: (y ^ 2, zl, k, zh, x))

    grad = ((R, D), F32)
    grad_x = call(final_kernel, [grad], images, gx_near[0], gx_plus, gx_minus, gx_far, name="unproject")[0]
    grad_y = call(final_kernel, [grad], texts, gy_near[0], gy_plus, gy_minus, gy_far, name="unproject")[0]
    loss = pl.pallas_call(
        loss_kernel,
        in_specs=[VMEM] * 2 + [pl.BlockSpec(memory_space=pl.ANY)] * 2,
        out_specs=SMEM,
        out_shape=jax.ShapeDtypeStruct((1,), F32),
        compiler_params=pltpu.CompilerParams(vmem_limit_bytes=1 << 20),
        name="loss",
    )(loss, step, grad_x, grad_y)
    return loss, grad_x, grad_y


def solution(mesh):
    return jax.shard_map(
        local,
        mesh=mesh,
        in_specs=(P(("row", "col"), None), P(("col", "row"), None), P(("row", "col")), P(), P()),
        out_specs=(P(), P(("row", "col"), None), P(("col", "row"), None)),
        check_vma=False,
    )
```
